32 devices in a mesh: groups: 2 (over y), space: 4 (over z), dp: 4 (over x, core).
Axes of the slice: x: 2, y: 2, z: 4, core: 2. Of those that a mesh axis runs over, the one named last changes fastest.
Arguments:
- features: bfloat16 [8, 6144, 64], P(('groups', 'dp'), 'space'), parts along dimension 0, may hold values from -6 to 6
- kernel_map: int32 [8, 27, 6144], P(('groups', 'dp'), None, 'space'), parts along dimension 0, may hold values from 0 to 2560, as said below
- child_map: int32 [8, 8, 1536], P(('groups', 'dp'), None, 'space'), parts along dimension 0, may hold values from 0 to 2048, as said below
- live_rows: int32 [8, 4], P(('groups', 'dp'), 'space'), parts along dimension 0, may hold values from 768 to 1536, as said below
- weight_first: bfloat16 [27, 64, 64], replicated, may hold values from -0.15625 to 0.15625
- weight_second: bfloat16 [27, 64, 64], replicated, may hold values from -0.15625 to 0.15625
- weight_down: bfloat16 [8, 64, 128], replicated, may hold values from -0.25 to 0.25
- out_grad: bfloat16 [8, 1536, 128], P(('groups', 'dp'), 'space'), parts along dimension 0, may hold values from -6 to 6
Outputs:
- coarse_features: bfloat16 [8, 1536, 128], P(('groups', 'dp'), 'space'), parts along dimension 0
- feature_grad: bfloat16 [8, 6144, 64], P(('groups', 'dp'), 'space'), parts along dimension 0
- grad_first: bfloat16 [54, 64, 64], P('groups'), parts along dimension 0
- grad_second: bfloat16 [54, 64, 64], P('groups'), parts along dimension 0
- grad_down: bfloat16 [16, 64, 128], P('groups'), parts along dimension 0
The draws below stay inside these ranges and needn't reach their ends.
There are 2 independent parts, one for each index of `groups`. The reference program is written for one: setup_inputs(seed, part) draws one part's arguments, and reference() takes and returns one part's arrays. A program takes and returns all parts, laid end to end along the dimension named above; an argument that names none is the same for every part. Nothing has to cross between parts.
Inputs may be any that keep to these rules, and one draw needn't show every extreme that they name: `kernel_map`: entries equal to 2560 mean no input; offset 27 // 2 of a row below its device's live count reads that row itself; rows at or above the live count read nothing. `child_map`: entries equal to 2048 mean no child; child 0 is present unless it falls past the strip's end. `live_rows`: in every sample some device is full.
All inputs are finite; a program needn't handle non-finite values.
Results may differ from the reference program's by a relative error of at most 0.006.
Values may be sent and summed in bfloat16 or wider, within the bound.
No kernel may reach another device: no remote copies, remote signals or barrier semaphores. Data moves between devices by JAX's collectives and lax.ppermute only.
A program may use at most 128 MiB of HBM per device.

```python
import jax
import jax.numpy as jnp
from jax import lax

C = 64
C2 = 128
KV = 27
KS = 8
ROWS_DEV = 1536
HALO = 512
COARSE_DEV = 384
SAMPLES = 4
ROWS = 6144
COARSE = 1536
N_SPACE = 4


def live_counts(key):
    base = jax.random.fold_in(key, 11)
    first_key, second_key = jax.random.split(base)
    counts = jax.random.randint(first_key, (SAMPLES, N_SPACE), ROWS_DEV // 2, ROWS_DEV + 1)
    fullest = jax.random.randint(second_key, (SAMPLES, 1), 0, N_SPACE)
    place = jnp.arange(N_SPACE, dtype=jnp.int32)[None, :]
    return jnp.where(place == fullest, ROWS_DEV, counts).astype(jnp.int32)


def draw_live_rows(key, part):
    return live_counts(key)


def draw_kernel_map(key, part):
    live = live_counts(key)
    key = jax.random.fold_in(key, 3)
    shift_key, keep_key = jax.random.split(key)
    rows = jnp.arange(ROWS, dtype=jnp.int32)
    device = rows // ROWS_DEV
    local = rows % ROWS_DEV
    alive = local[None, :] < live[:, device]
    centre = (jnp.arange(KV, dtype=jnp.int32) == KV // 2)[None, :, None]
    shift = jax.random.randint(shift_key, (SAMPLES, KV, ROWS), -HALO, HALO + 1)
    shift = jnp.where(centre, 0, shift)
    keep = (jax.random.randint(keep_key, (SAMPLES, KV, ROWS), 0, 2) == 1) | centre
    spot = local[None, None, :] + HALO + shift
    whole = device[None, None, :] * ROWS_DEV - HALO + spot
    inside = (whole >= 0) & (whole < ROWS)
    valid = keep & alive[:, None, :] & inside
    return jnp.where(valid, spot, ROWS_DEV + 2 * HALO).astype(jnp.int32)


def draw_child_map(key, part):
    key = jax.random.fold_in(key, 5)
    place_key, keep_key = jax.random.split(key)
    crow = jnp.arange(COARSE, dtype=jnp.int32)
    device = crow // COARSE_DEV
    local = crow % COARSE_DEV
    spot = 4 * local[None, None, :] + jax.random.randint(place_key, (SAMPLES, KS, COARSE), 0, HALO + 1)
    firstborn = (jnp.arange(KS, dtype=jnp.int32) == 0)[None, :, None]
    keep = (jax.random.randint(keep_key, (SAMPLES, KS, COARSE), 0, 2) == 1) | firstborn
    inside = device[None, None, :] * ROWS_DEV + spot < ROWS
    return jnp.where(keep & inside, spot, ROWS_DEV + HALO).astype(jnp.int32)


def steps_of(rng, shape, cuts, low, high):
    level = 1.0
    for position, parts in cuts:
        steps = jax.random.uniform(jax.random.fold_in(jax.random.fold_in(rng, 6), position), (parts,), jnp.float32, low / len(cuts), high / len(cuts))
        level = level * jnp.repeat(jnp.exp(steps), shape[position] // parts).reshape((-1,) + (1,) * (len(shape) - 1 - position))
    return level


def gaussian(rng, extent, scale, reach, cuts=(), kind=jnp.bfloat16):
    result = jax.random.normal(rng, extent, jnp.float32) * scale
    if len(cuts) > 0:
        result = steps_of(rng, extent, cuts, -0.22, 0.18) * result
    return jnp.clip(result, min=-reach, max=reach).astype(kind)


def setup_inputs(seed: int = 0, part: int = 0) -> dict:
    arg_keys = jax.random.split(jax.random.key(seed), 9)
    part_splits = jax.random.split(jax.random.fold_in(arg_keys[8], part), 9)
    return {
        "features": gaussian(part_splits[0], (SAMPLES, ROWS, C), 1.0, 6.0, ((0, 4), (1, 4))),
        "kernel_map": draw_kernel_map(jax.random.fold_in(jax.random.fold_in(arg_keys[8], part), 71), part),
        "child_map": draw_child_map(jax.random.fold_in(jax.random.fold_in(arg_keys[8], part), 71), part),
        "live_rows": draw_live_rows(jax.random.fold_in(jax.random.fold_in(arg_keys[8], part), 71), part),
        "weight_first": gaussian(arg_keys[4], (KV, C, C), (KV * C) ** -0.5, 0.15625),
        "weight_second": gaussian(arg_keys[5], (KV, C, C), (KV * C) ** -0.5, 0.15625),
        "weight_down": gaussian(arg_keys[6], (KS, C, C2), (KS * C) ** -0.5, 0.25),
        "out_grad": gaussian(part_splits[7], (SAMPLES, COARSE, C2), 1.0, 6.0, ((0, 4), (1, 4))),
    }


def silu_slope(value):
    sig = jax.nn.sigmoid(value)
    return sig * (1.0 + value * (1.0 - sig))


def padded_rows(field):
    return jnp.concatenate([field, jnp.zeros((1, field.shape[1]), field.dtype)], axis=0)


def conv_rows(field, sources, weights):
    padded = padded_rows(field)

    def step(total, item):
        source, weight = item
        return total + jnp.dot(padded[source], weight, preferred_element_type=jnp.float32), None

    start = jnp.zeros((sources.shape[1], weights.shape[2]), jnp.float32)
    total, unused = lax.scan(step, start, (sources, weights))
    return total


def conv_back(grad, sources, weights, count):
    def step(total, item):
        source, weight = item
        return total.at[source].add(jnp.dot(grad, weight.T, preferred_element_type=jnp.float32)), None

    start = jnp.zeros((count + 1, weights.shape[1]), jnp.float32)
    total, unused = lax.scan(step, start, (sources, weights))
    return total[:count]


def weight_terms(field, sources, grad):
    padded = padded_rows(field)
    return lax.map(lambda source: jnp.dot(padded[source].T, grad, preferred_element_type=jnp.float32), sources)


def one_sample(feats, kmap, cmap, live, weight_first, weight_second, weight_down, grad_out):
    rows = jnp.arange(ROWS, dtype=jnp.int32)
    device = rows // ROWS_DEV
    spot = device[None, :] * ROWS_DEV - HALO + kmap
    sources = jnp.where((kmap < ROWS_DEV + 2 * HALO) & (spot >= 0) & (spot < ROWS), spot, ROWS).astype(jnp.int32)
    crow = jnp.arange(COARSE, dtype=jnp.int32)
    cdevice = crow // COARSE_DEV
    cspot = cdevice[None, :] * ROWS_DEV + cmap
    csources = jnp.where((cmap < ROWS_DEV + HALO) & (cspot < ROWS), cspot, ROWS).astype(jnp.int32)
    alive = ((rows % ROWS_DEV) < live[device]).astype(jnp.float32)[:, None]
    pre_first = conv_rows(feats, sources, weight_first)
    first = (jax.nn.silu(pre_first) * alive).astype(jnp.bfloat16)
    pre_second = conv_rows(first, sources, weight_second) + feats.astype(jnp.float32)
    second = (jax.nn.silu(pre_second) * alive).astype(jnp.bfloat16)
    coarse = conv_rows(second, csources, weight_down).astype(jnp.bfloat16)
    grad_second_rows = conv_back(grad_out, csources, weight_down, ROWS)
    grad_down = weight_terms(second, csources, grad_out)
    d_second = (grad_second_rows * silu_slope(pre_second) * alive).astype(jnp.bfloat16)
    grad_first_rows = conv_back(d_second, sources, weight_second, ROWS)
    grad_second = weight_terms(first, sources, d_second)
    d_first = (grad_first_rows * silu_slope(pre_first) * alive).astype(jnp.bfloat16)
    feature_rows = conv_back(d_first, sources, weight_first, ROWS)
    grad_first = weight_terms(feats, sources, d_first)
    feature_grad = (feature_rows + d_second.astype(jnp.float32)).astype(jnp.bfloat16)
    return coarse, feature_grad, grad_first, grad_second, grad_down


def reference(features, kernel_map, child_map, live_rows, weight_first, weight_second, weight_down, out_grad):
    def run(items):
        feats, kmap, cmap, live, grad_out = items
        return one_sample(feats, kmap, cmap, live, weight_first, weight_second, weight_down, grad_out)

    coarse, feature_grad, grad_first, grad_second, grad_down = lax.map(run, (features, kernel_map, child_map, live_rows, out_grad))
    scale = (SAMPLES * ROWS) ** -0.5
    grad_first = (jnp.sum(grad_first, axis=0) * scale).astype(jnp.bfloat16)
    grad_second = (jnp.sum(grad_second, axis=0) * scale).astype(jnp.bfloat16)
    grad_down = (jnp.sum(grad_down, axis=0) * scale).astype(jnp.bfloat16)
    return coarse, feature_grad, grad_first, grad_second, grad_down
```

```python
import functools

import jax
import jax.numpy as jnp
from jax import lax
from jax.experimental import pallas as pl
from jax.experimental.pallas import tpu as pltpu
from jax.sharding import PartitionSpec as P

HALO = 512
SLABS = 4
VMEM_BYTES = 48 * 2**20


def silu_slope(value):
    sig = jax.nn.sigmoid(value)
    return sig * (1.0 + value * (1.0 - sig))


def split_index(index, span):
    slab = sum((index >= (s * span)).astype(jnp.int32) for s in range(1, SLABS))
    return slab, index - slab * span


def one_hot(place, span):
    shape = (span, place.shape[1])
    here = jnp.broadcast_to(place, shape).astype(jnp.int16)
    return jnp.where(
        here == lax.broadcasted_iota(jnp.int16, shape, 0), jnp.bfloat16(1), jnp.bfloat16(0)
    )


def slab_diagonal(weight):
    rows, cols = weight.shape
    tiled = jnp.concatenate([jnp.concatenate([weight] * SLABS, axis=1)] * SLABS, axis=0)
    row = lax.broadcasted_iota(jnp.int32, tiled.shape, 0) // rows
    col = lax.broadcasted_iota(jnp.int32, tiled.shape, 1) // cols
    return jnp.where(row == col, tiled, jnp.zeros_like(tiled))


def fill_slabs(slabs_ref, pieces):
    chans = pieces[0].shape[0]
    span = slabs_ref.shape[1]
    slab, at = 0, 0
    for piece in pieces:
        done = 0
        while done < piece.shape[1]:
            take = min(span - at, piece.shape[1] - done)
            slabs_ref[slab * chans : (slab + 1) * chans, at : at + take] = piece[:, done : done + take]
            done, at = done + take, at + take
            if at == span:
                slab, at = slab + 1, 0


def window_of(slabs, begin, end):
    chans = slabs.shape[0] // SLABS
    span = slabs.shape[1]
    pieces = []
    while begin < end:
        slab, at = divmod(begin, span)
        take = min(span - at, end - begin)
        pieces.append(slabs[slab * chans : (slab + 1) * chans, at : at + take])
        begin += take
    return pieces[0] if len(pieces) == 1 else jnp.concatenate(pieces, axis=1)


def fold(stacked):
    chans = stacked.shape[0] // SLABS
    return sum(stacked[s * chans : (s + 1) * chans] for s in range(SLABS))


def nt(left, right):
    return lax.dot_general(
        left, right, (((1,), (1,)), ((), ())), preferred_element_type=jnp.float32
    )


def conv(map_ref, weight_ref, slabs_ref, total_ref):
    span, rows = slabs_ref.shape[1], total_ref.shape[1]
    chans = slabs_ref.shape[0] // SLABS
    owner = lax.broadcasted_iota(jnp.int32, (SLABS * chans, rows), 0) // chans
    total_ref[...] = jnp.zeros_like(total_ref)

    def step(k, carry):
        values = jnp.dot(
            slab_diagonal(weight_ref[k].T), slabs_ref[...], preferred_element_type=jnp.float32
        ).astype(jnp.bfloat16)
        slab, place = split_index(map_ref[k], span)
        read = jnp.dot(values, one_hot(place, span), preferred_element_type=jnp.float32)
        total_ref[...] += jnp.where(slab == owner, read, 0.0)
        return carry

    lax.fori_loop(0, map_ref.shape[0], step, 0)
    return fold(total_ref[...])


def conv_back(map_ref, weight_ref, slabs_ref, grad_ref, spread_ref, total_ref, weight_grad_ref):
    span = slabs_ref.shape[1]
    chans = grad_ref.shape[0]
    row = lax.broadcasted_iota(jnp.int32, (SLABS * chans, SLABS * chans), 0) // chans
    col = lax.broadcasted_iota(jnp.int32, (SLABS * chans, SLABS * chans), 1) // chans
    total_ref[...] = jnp.zeros_like(total_ref)

    def step(k, carry):
        slab, place = split_index(map_ref[k], span)
        grad = grad_ref[...]
        for s in range(SLABS):
            spread_ref[s * chans : (s + 1) * chans, :] = jnp.where(
                slab == s, grad, jnp.zeros_like(grad)
            )
        sums = nt(spread_ref[...], one_hot(place, span)).astype(jnp.bfloat16)
        total_ref[...] += jnp.dot(
            slab_diagonal(weight_ref[k]), sums, preferred_element_type=jnp.float32
        )
        pairs = fold(jnp.where(row == col, nt(slabs_ref[...], sums), 0.0))
        weight_grad_ref[k] = sum(pairs[:, s * chans : (s + 1) * chans] for s in range(SLABS))
        return carry

    lax.fori_loop(0, map_ref.shape[0], step, 0)


def live_mask(live_ref, rows):
    return lax.broadcasted_iota(jnp.int32, (1, rows), 1) < live_ref[0, 0]


def spread_kernel(child_ref, down_ref, grad_ref, own_ref, next_ref):
    kids, chans, wide = down_ref.shape
    coarse = grad_ref.shape[0]
    rows = own_ref.shape[1]
    span = (rows + HALO) // SLABS
    total = jnp.zeros((SLABS * chans, span), jnp.float32)
    terms = nt(down_ref[...].reshape(kids * chans, wide), grad_ref[...]).astype(jnp.bfloat16)
    for j in range(kids):
        slab, place = split_index(child_ref[j : j + 1, :], span)
        term = terms[j * chans : (j + 1) * chans]
        apart = jnp.concatenate(
            [jnp.where(slab == s, term, jnp.zeros_like(term)) for s in range(SLABS)], axis=0
        )
        total += nt(apart, one_hot(place, span))
    own_ref[...] = window_of(total, 0, rows)
    next_ref[...] = window_of(total, rows, rows + HALO).astype(next_ref.dtype)


def first_kernel(
    live_ref, map_ref, weight_ref, field_ref, prev_ref, next_ref, first_ref, slope_ref, slabs_ref, total_ref
):
    fill_slabs(slabs_ref, [prev_ref, field_ref, next_ref])
    pre = conv(map_ref, weight_ref, slabs_ref, total_ref)
    alive = live_mask(live_ref, pre.shape[1])
    first_ref[...] = jnp.where(alive, jax.nn.silu(pre), 0.0).astype(jnp.bfloat16)
    slope_ref[...] = jnp.where(alive, silu_slope(pre), 0.0)


def second_kernel(
    live_ref,
    map_ref,
    weight_ref,
    first_ref,
    prev_ref,
    next_ref,
    field_ref,
    rows_ref,
    returned_ref,
    second_ref,
    d_second_ref,
    own_ref,
    to_prev_ref,
    to_next_ref,
    weight_grad_ref,
    slabs_ref,
    total_ref,
    spread_ref,
    sums_ref,
):
    fill_slabs(slabs_ref, [prev_ref, first_ref, next_ref])
    pre = conv(map_ref, weight_ref, slabs_ref, total_ref) + field_ref[...].astype(jnp.float32)
    rows = pre.shape[1]
    alive = live_mask(live_ref, rows)
    second_ref[...] = jnp.where(alive, jax.nn.silu(pre), 0.0).astype(jnp.bfloat16)
    slope = jnp.where(alive, silu_slope(pre), 0.0)
    head = rows_ref[:, :HALO] + returned_ref[...].astype(jnp.float32)
    grad_rows = jnp.concatenate([head, rows_ref[:, HALO:]], axis=1)
    d_second_ref[...] = (grad_rows * slope).astype(jnp.bfloat16)
    conv_back(map_ref, weight_ref, slabs_ref, d_second_ref, spread_ref, sums_ref, weight_grad_ref)
    sums = sums_ref[...]
    own_ref[...] = window_of(sums, HALO, HALO + rows)
    to_prev_ref[...] = window_of(sums, 0, HALO).astype(to_prev_ref.dtype)
    to_next_ref[...] = window_of(sums, HALO + rows, 2 * HALO + rows).astype(to_next_ref.dtype)


def down_kernel(child_ref, down_ref, grad_ref, second_ref, next_ref, coarse_ref, grad_down_ref, slabs_ref, taken_ref):
    kids, chans, wide = down_ref.shape
    fill_slabs(slabs_ref, [second_ref, next_ref])
    span = slabs_ref.shape[1]
    owner = lax.broadcasted_iota(jnp.int32, (SLABS * chans, grad_ref.shape[0]), 0) // chans
    for j in range(kids):
        slab, place = split_index(child_ref[j : j + 1, :], span)
        read = jnp.dot(slabs_ref[...], one_hot(place, span), preferred_element_type=jnp.float32)
        taken_ref[j * chans : (j + 1) * chans, :] = fold(
            jnp.where(slab == owner, read, 0.0)
        ).astype(jnp.bfloat16)
    taken = taken_ref[...]
    flat = down_ref[...].reshape(kids * chans, wide)
    coarse_ref[...] = jnp.dot(taken.T, flat, preferred_element_type=jnp.float32).astype(jnp.bfloat16)
    grad_down_ref[...] = jnp.dot(
        taken, grad_ref[...], preferred_element_type=jnp.float32
    ).reshape(grad_down_ref.shape)


def back_kernel(
    map_ref,
    weight_ref,
    field_ref,
    prev_ref,
    next_ref,
    rows_ref,
    from_prev_ref,
    from_next_ref,
    slope_ref,
    own_ref,
    to_prev_ref,
    to_next_ref,
    weight_grad_ref,
    slabs_ref,
    grad_ref,
    spread_ref,
    sums_ref,
):
    rows = rows_ref.shape[1]
    fill_slabs(slabs_ref, [prev_ref, field_ref, next_ref])
    grad_ref[...] = (
        jnp.concatenate(
            [
                rows_ref[:, :HALO] + from_prev_ref[...].astype(jnp.float32),
                rows_ref[:, HALO : rows - HALO],
                rows_ref[:, rows - HALO :] + from_next_ref[...].astype(jnp.float32),
            ],
            axis=1,
        )
        * slope_ref[...]
    ).astype(jnp.bfloat16)
    conv_back(map_ref, weight_ref, slabs_ref, grad_ref, spread_ref, sums_ref, weight_grad_ref)
    sums = sums_ref[...]
    own_ref[...] = window_of(sums, HALO, HALO + rows)
    to_prev_ref[...] = window_of(sums, 0, HALO).astype(to_prev_ref.dtype)
    to_next_ref[...] = window_of(sums, HALO + rows, 2 * HALO + rows).astype(to_next_ref.dtype)


def shape(dims, dtype):
    return jax.ShapeDtypeStruct(dims, dtype)


def call(kernel, outs, scratch, flops, *args):
    smem = pl.BlockSpec(memory_space=pltpu.SMEM)
    vmem = pl.BlockSpec(memory_space=pltpu.VMEM)
    return pl.pallas_call(
        kernel,
        out_shape=outs,
        in_specs=[smem if a.shape == (1, 1) else vmem for a in args],
        out_specs=[vmem] * len(outs),
        scratch_shapes=scratch,
        compiler_params=pltpu.CompilerParams(vmem_limit_bytes=VMEM_BYTES),
        cost_estimate=pl.CostEstimate(flops=flops, bytes_accessed=2**20, transcendentals=0),
    )(*args)


def to_following(value):
    count = lax.axis_size("space")
    return lax.ppermute(value, "space", [(i, i + 1) for i in range(count - 1)])


def to_preceding(value):
    count = lax.axis_size("space")
    return lax.ppermute(value, "space", [(i + 1, i) for i in range(count - 1)])


def sum_over_axes(value):
    for axis in ("dp", "space"):
        count = lax.axis_size(axis)
        if count > 4:
            value = lax.psum(value, axis)
            continue
        step = 1
        while step < count:
            sent = value.astype(jnp.bfloat16)
            value = value + lax.ppermute(sent, axis, [(i, i ^ step) for i in range(count)]).astype(
                jnp.float32
            )
            step *= 2
    return value


def body(
    features, kernel_map, child_map, live_rows, weight_first, weight_second, weight_down, out_grad
):
    field = features[0].T
    chans, rows = field.shape
    offsets = kernel_map.reshape(kernel_map.shape[1], 1, rows)
    count = offsets.shape[0]
    children = child_map[0]
    kids, coarse = children.shape
    wide = weight_down.shape[2]
    grad_out = out_grad[0]
    bf16, f32 = jnp.bfloat16, jnp.float32
    span = (rows + 2 * HALO) // SLABS
    down_span = (rows + HALO) // SLABS
    stack = SLABS * chans
    conv_flops = 2 * count * stack * span * rows

    prev_field = to_following(field[:, rows - HALO :])
    next_field = to_preceding(field[:, :HALO])
    grad_rows, spread_next = call(
        spread_kernel,
        [shape((chans, rows), f32), shape((chans, HALO), bf16)],
        [],
        2 * kids * stack * down_span * coarse,
        children,
        weight_down,
        grad_out,
    )
    returned = to_following(spread_next)
    first, slope = call(
        first_kernel,
        [shape((chans, rows), bf16), shape((chans, rows), f32)],
        [pltpu.VMEM((stack, span), bf16), pltpu.VMEM((stack, rows), f32)],
        conv_flops,
        live_rows,
        offsets,
        weight_first,
        field,
        prev_field,
        next_field,
    )
    prev_first = to_following(first[:, rows - HALO :])
    next_first = to_preceding(first[:, :HALO])
    second, d_second, own, to_prev, to_next, grad_second = call(
        second_kernel,
        [
            shape((chans, rows), bf16),
            shape((chans, rows), bf16),
            shape((chans, rows), f32),
            shape((chans, HALO), bf16),
            shape((chans, HALO), bf16),
            shape((count, chans, chans), f32),
        ],
        [
            pltpu.VMEM((stack, span), bf16),
            pltpu.VMEM((stack, rows), f32),
            pltpu.VMEM((stack, rows), bf16),
            pltpu.VMEM((stack, span), f32),
        ],
        2 * conv_flops,
        live_rows,
        offsets,
        weight_second,
        first,
        prev_first,
        next_first,
        field,
        grad_rows,
        returned,
    )
    from_next = to_preceding(to_prev)
    from_prev = to_following(to_next)
    next_second = to_preceding(second[:, :HALO])
    coarse_out, grad_down = call(
        down_kernel,
        [shape((coarse, wide), bf16), shape((kids, chans, wide), f32)],
        [pltpu.VMEM((stack, down_span), bf16), pltpu.VMEM((kids * chans, coarse), bf16)],
        2 * kids * stack * down_span * coarse,
        children,
        weight_down,
        grad_out,
        second,
        next_second,
    )
    own, to_prev, to_next, grad_first = call(
        back_kernel,
        [
            shape((chans, rows), f32),
            shape((chans, HALO), bf16),
            shape((chans, HALO), bf16),
            shape((count, chans, chans), f32),
        ],
        [
            pltpu.VMEM((stack, span), bf16),
            pltpu.VMEM((chans, rows), bf16),
            pltpu.VMEM((stack, rows), bf16),
            pltpu.VMEM((stack, span), f32),
        ],
        conv_flops,
        offsets,
        weight_first,
        field,
        prev_field,
        next_field,
        own,
        from_prev,
        from_next,
        slope,
    )
    from_next = to_preceding(to_prev).astype(f32)
    from_prev = to_following(to_next).astype(f32)
    total = own + d_second.astype(f32)
    total = total.at[:, :HALO].add(from_prev)
    total = total.at[:, rows - HALO :].add(from_next)
    feature_grad = total.astype(bf16).T
    scale = float(lax.axis_size("dp") * lax.axis_size("space") * rows) ** (-0.5)
    flat = jnp.concatenate(
        [grad_second.reshape(-1, wide), grad_down.reshape(-1, wide)], axis=0
    )
    flat = (sum_over_axes(flat) * scale).astype(bf16)
    cut = grad_second.size // wide
    out_second = flat[:cut].reshape(grad_second.shape)
    out_down = flat[cut:].reshape(grad_down.shape)
    out_first = (sum_over_axes(grad_first) * scale).astype(bf16)
    return (coarse_out[None], feature_grad[None], out_first, out_second, out_down)


def solution(mesh):
    placed = (
        P(("groups", "dp"), "space", None),
        P(("groups", "dp"), None, "space"),
        P(("groups", "dp"), None, "space"),
        P(("groups", "dp"), "space"),
        P(),
        P(),
        P(),
        P(("groups", "dp"), "space", None),
    )
    return jax.shard_map(
        body,
        mesh=mesh,
        in_specs=placed,
        out_specs=(
            P(("groups", "dp"), "space", None),
            P(("groups", "dp"), "space", None),
            P("groups", None, None),
            P("groups", None, None),
            P("groups", None, None),
        ),
        check_vma=False,
    )
```

```python
import jax
import jax.numpy as jnp
from jax import lax
from jax.experimental import pallas as pl
from jax.experimental.pallas import tpu as pltpu
from jax.sharding import PartitionSpec as P

HALO = 512
READ_SPAN = 512
SPREAD_SPAN = 256
DOWN_SPAN = 512
UNROLL = 9
VMEM_BYTES = 40 * 2**20
LIVE, FIRST, LAST, DP = range(4)


def silu_slope(value):
    sig = jax.nn.sigmoid(value)
    return sig * (1.0 + value * (1.0 - sig))


def locate(index, span):
    slab = lax.shift_right_arithmetic(index, span.bit_length() - 1)
    return slab, jnp.where(index >= 0, index & (span - 1), -1)


def one_hot(place, span):
    shape = (span, place.shape[1])
    here = jnp.broadcast_to(place, shape).astype(jnp.int16)
    return jnp.where(
        here == lax.broadcasted_iota(jnp.int16, shape, 0), jnp.bfloat16(1), jnp.bfloat16(0)
    )


def nt(left, right):
    return lax.dot_general(
        left, right, (((1,), (1,)), ((), ())), preferred_element_type=jnp.float32
    )


def nn(left, right):
    return jnp.dot(left, right, preferred_element_type=jnp.float32)


def read_rows(slabs, index, chans):
    count, span = slabs.shape[0] // chans, slabs.shape[1]
    slab, place = locate(index, span)
    read = nn(slabs, one_hot(place, span))
    picked = read[(count - 1) * chans :]
    for s in range(count - 1):
        picked = jnp.where(slab == s, read[s * chans : (s + 1) * chans], picked)
    return picked.astype(jnp.bfloat16)


def spread_rows(terms_ref, terms, index, count, span):
    chans = terms.shape[0]
    slab, place = locate(index, span)
    for s in range(count):
        terms_ref[s * chans : (s + 1) * chans, :] = jnp.where(slab == s, terms, jnp.zeros_like(terms))
    return nt(terms_ref[...], one_hot(place, span))


def conv(map_ref, weight_ref, slabs_ref, taken_ref):
    count, chans = weight_ref.shape[0], weight_ref.shape[1]
    rows = taken_ref.shape[1]
    window = rows + 2 * HALO

    def step(k, carry):
        index = map_ref[k]
        index = jnp.where(index < window, index, -1)
        at = pl.ds(pl.multiple_of(k * chans, chans), chans)
        for begin in range(0, rows, HALO):
            part = slice(begin, begin + HALO)
            taken_ref[at, part] = read_rows(slabs_ref[...], index[:, part], chans)
        return carry

    lax.fori_loop(0, count, step, 0, unroll=UNROLL)
    weights = weight_ref[...].reshape(count * chans, -1).T
    return nn(weights, taken_ref[...])


def side_by_side(weight_ref):
    return jnp.concatenate([weight_ref[k] for k in range(weight_ref.shape[0])], axis=1)


def conv_back(map_ref, weight_ref, grad_ref, terms_ref, sums_ref, halo):
    count, chans = weight_ref.shape[0], weight_ref.shape[1]
    rows = grad_ref.shape[1]
    slabs = sums_ref.shape[0]

    def step(k, carry):
        index = map_ref[k]
        if halo:
            after = (index >= HALO + rows) & (index < 2 * HALO + rows)
            index = jnp.where(after, index - rows, jnp.where(index < HALO, index, -1))
        else:
            index = jnp.where(index < HALO + rows, index - HALO, -1)
        sums = spread_rows(terms_ref, grad_ref[...], index, slabs, SPREAD_SPAN).astype(jnp.bfloat16)
        at = pl.ds(pl.multiple_of(k * chans, chans), chans)
        for s in range(slabs):
            sums_ref[s, at, :] = sums[s * chans : (s + 1) * chans]
        return carry

    lax.fori_loop(0, count, step, 0, unroll=UNROLL)
    weights = side_by_side(weight_ref)
    return [nn(weights, sums_ref[s]) for s in range(slabs)]


def put_window(slabs_ref, info_ref, before, own_ref, after):
    chans, rows = own_ref.shape
    zero = jnp.zeros_like(before)
    slabs_ref[:chans, :] = jnp.where(info_ref[0, FIRST] == 1, zero, before)
    for s in range(rows // READ_SPAN):
        slabs_ref[(s + 1) * chans : (s + 2) * chans, :] = own_ref[:, s * READ_SPAN : (s + 1) * READ_SPAN]
    last = rows // READ_SPAN + 1
    slabs_ref[last * chans : (last + 1) * chans, :] = jnp.where(info_ref[0, LAST] == 1, zero, after)


def live_mask(info_ref, rows):
    return lax.broadcasted_iota(jnp.int32, (1, rows), 1) < info_ref[0, LIVE]


def add_ends(info_ref, rows_ref, before, after):
    rows = rows_ref.shape[1]
    before = jnp.where(info_ref[0, FIRST] == 1, 0.0, before.astype(jnp.float32))
    after = jnp.where(info_ref[0, LAST] == 1, 0.0, after.astype(jnp.float32))
    return jnp.concatenate(
        [
            rows_ref[:, :HALO] + before,
            rows_ref[:, HALO : rows - HALO],
            rows_ref[:, rows - HALO :] + after,
        ],
        axis=1,
    )


def spread_kernel(child_ref, down_ref, grad_ref, own_ref, next_ref, terms_ref):
    kids, chans, wide = down_ref.shape
    coarse = grad_ref.shape[0]
    rows = own_ref.shape[1]
    slabs = (rows + HALO) // DOWN_SPAN
    total = jnp.zeros((slabs * chans, DOWN_SPAN), jnp.float32)
    terms = nt(down_ref[...].reshape(kids * chans, wide), grad_ref[...]).astype(jnp.bfloat16)
    for j in range(kids):
        index = child_ref[j : j + 1, :]
        index = jnp.where(index < rows + HALO, index, -1)
        total += spread_rows(terms_ref, terms[j * chans : (j + 1) * chans], index, slabs, DOWN_SPAN)
    for s in range(slabs - 1):
        own_ref[:, s * DOWN_SPAN : (s + 1) * DOWN_SPAN] = total[s * chans : (s + 1) * chans]
    next_ref[...] = total[(slabs - 1) * chans :].astype(next_ref.dtype)


def first_kernel(
    info_ref,
    map_ref,
    weight_ref,
    field_ref,
    before_ref,
    after_ref,
    spread_ref,
    first_ref,
    slope_ref,
    taken_ref,
    to_next_ref,
    slabs_ref,
):
    put_window(slabs_ref, info_ref, before_ref[...], field_ref, after_ref[...])
    pre = conv(map_ref, weight_ref, slabs_ref, taken_ref)
    chans, rows = pre.shape
    alive = live_mask(info_ref, rows)
    first_ref[...] = jnp.where(alive, jax.nn.silu(pre), 0.0).astype(jnp.bfloat16)
    slope_ref[...] = jnp.where(alive, silu_slope(pre), 0.0)
    to_next_ref[:chans] = first_ref[:, rows - HALO :]
    to_next_ref[chans:] = spread_ref[...]


def second_kernel(
    info_ref,
    map_ref,
    weight_ref,
    first_ref,
    before_ref,
    after_ref,
    field_ref,
    rows_ref,
    second_ref,
    d_second_ref,
    grad_weight_ref,
    to_prev_ref,
    to_next_ref,
    slabs_ref,
    taken_ref,
    terms_ref,
    sums_ref,
):
    chans, rows = first_ref.shape
    put_window(slabs_ref, info_ref, before_ref[:chans], first_ref, after_ref[...])
    pre = conv(map_ref, weight_ref, slabs_ref, taken_ref) + field_ref[...].astype(jnp.float32)
    alive = live_mask(info_ref, rows)
    second_ref[...] = jnp.where(alive, jax.nn.silu(pre), 0.0).astype(jnp.bfloat16)
    slope = jnp.where(alive, silu_slope(pre), 0.0)
    returned = jnp.where(info_ref[0, FIRST] == 1, 0.0, before_ref[chans:].astype(jnp.float32))
    grad_rows = jnp.concatenate([rows_ref[:, :HALO] + returned, rows_ref[:, HALO:]], axis=1)
    d_second_ref[...] = (grad_rows * slope).astype(jnp.bfloat16)
    grad_weight_ref[...] = nt(d_second_ref[...], taken_ref[...])
    ends = conv_back(map_ref, weight_ref, d_second_ref, terms_ref, sums_ref, True)
    half = len(ends) // 2
    to_prev_ref[:chans] = jnp.concatenate(ends[:half], axis=1).astype(to_prev_ref.dtype)
    to_prev_ref[chans:] = second_ref[:, :HALO]
    to_next_ref[...] = jnp.concatenate(ends[half:], axis=1).astype(to_next_ref.dtype)


def own_kernel(map_ref, weight_ref, grad_ref, own_ref, terms_ref, sums_ref):
    parts = conv_back(map_ref, weight_ref, grad_ref, terms_ref, sums_ref, False)
    for s, part in enumerate(parts):
        own_ref[:, s * SPREAD_SPAN : (s + 1) * SPREAD_SPAN] = part


def ends_kernel(map_ref, weight_ref, grad_ref, to_prev_ref, to_next_ref, terms_ref, sums_ref):
    ends = conv_back(map_ref, weight_ref, grad_ref, terms_ref, sums_ref, True)
    half = len(ends) // 2
    to_prev_ref[...] = jnp.concatenate(ends[:half], axis=1).astype(to_prev_ref.dtype)
    to_next_ref[...] = jnp.concatenate(ends[half:], axis=1).astype(to_next_ref.dtype)


def middle_kernel(
    info_ref,
    child_ref,
    down_ref,
    grad_ref,
    second_ref,
    from_next_ref,
    from_prev_ref,
    rows_ref,
    slope_ref,
    taken_ref,
    grad_second_ref,
    coarse_ref,
    d_first_ref,
    grads_ref,
    slabs_ref,
    kids_ref,
):
    kids, chans, wide = down_ref.shape
    rows = second_ref.shape[1]
    for s in range(rows // DOWN_SPAN):
        slabs_ref[s * chans : (s + 1) * chans, :] = second_ref[:, s * DOWN_SPAN : (s + 1) * DOWN_SPAN]
    after = from_next_ref[chans:]
    slabs_ref[rows // DOWN_SPAN * chans :, :] = jnp.where(
        info_ref[0, LAST] == 1, jnp.zeros_like(after), after
    )
    for j in range(kids):
        index = child_ref[j : j + 1, :]
        index = jnp.where(index < rows + HALO, index, -1)
        kids_ref[j * chans : (j + 1) * chans, :] = read_rows(slabs_ref[...], index, chans)
    taken = kids_ref[...]
    flat = down_ref[...].reshape(kids * chans, wide)
    coarse_ref[...] = nn(taken.T, flat).astype(jnp.bfloat16)
    grad_down = nn(taken, grad_ref[...])
    d_first_ref[...] = (
        add_ends(info_ref, rows_ref, from_prev_ref[...], from_next_ref[:chans]) * slope_ref[...]
    ).astype(jnp.bfloat16)
    size = grad_second_ref.shape[1]
    grads_ref[:, :size] = grad_second_ref[...]
    grads_ref[:, size : 2 * size] = nt(d_first_ref[...], taken_ref[...])
    for j in range(kids):
        grads_ref[:, 2 * size + j * wide : 2 * size + (j + 1) * wide] = grad_down[
            j * chans : (j + 1) * chans
        ]


def last_kernel(info_ref, own_ref, d_second_ref, before_ref, after_ref, grads_ref, field_ref, first_ref, second_ref, down_ref):
    total = add_ends(info_ref, own_ref, before_ref[...], after_ref[...])
    field_ref[...] = (total + d_second_ref[...].astype(jnp.float32)).astype(jnp.bfloat16)
    count, chans = first_ref.shape[0], first_ref.shape[1]
    kids, wide = down_ref.shape[0], down_ref.shape[2]
    size = count * chans
    second = grads_ref[:, :size].T
    first = grads_ref[:, size : 2 * size].T
    for k in range(count):
        second_ref[k] = second[k * chans : (k + 1) * chans]
        first_ref[k] = first[k * chans : (k + 1) * chans]
    for j in range(kids):
        down_ref[j] = grads_ref[:, 2 * size + j * wide : 2 * size + (j + 1) * wide]


def shape(dims, dtype):
    return jax.ShapeDtypeStruct(dims, dtype)


def call(kernel, outs, scratch, flops, *args):
    smem = pl.BlockSpec(memory_space=pltpu.SMEM)
    vmem = pl.BlockSpec(memory_space=pltpu.VMEM)
    return pl.pallas_call(
        kernel,
        out_shape=outs,
        in_specs=[smem if a.shape == (1, 4) else vmem for a in args],
        out_specs=[vmem] * len(outs),
        scratch_shapes=scratch,
        compiler_params=pltpu.CompilerParams(vmem_limit_bytes=VMEM_BYTES),
        cost_estimate=pl.CostEstimate(flops=flops, bytes_accessed=2**20, transcendentals=0),
    )(*args)


def shifted(value, axis, steps):
    count = lax.axis_size(axis)
    return lax.ppermute(value, axis, [(i, (i + steps) % count) for i in range(count)])


def body(
    features, kernel_map, child_map, live_rows, weight_first, weight_second, weight_down, out_grad
):
    bf16, f32 = jnp.bfloat16, jnp.float32
    field = features[0].T
    chans, rows = field.shape
    count = kernel_map.shape[1]
    offsets = kernel_map.reshape(count, 1, rows)
    children = child_map[0]
    kids, coarse = children.shape
    wide = weight_down.shape[2]
    grad_out = out_grad[0]
    place = lax.axis_index("space")
    devices = lax.axis_size("space")
    info = jnp.stack(
        [
            live_rows[0, 0],
            (place == 0).astype(jnp.int32),
            (place == devices - 1).astype(jnp.int32),
            lax.axis_index("dp").astype(jnp.int32),
        ]
    ).reshape(1, 4)
    window = rows + 2 * HALO
    flops = 2 * count * window * chans * rows
    down_slabs = (rows + HALO) // DOWN_SPAN
    end_slabs, own_slabs = 2 * HALO // SPREAD_SPAN, rows // SPREAD_SPAN
    slabs_scratch = pltpu.VMEM((window // READ_SPAN * chans, READ_SPAN), bf16)
    end_scratch = [
        pltpu.VMEM((end_slabs * chans, rows), bf16),
        pltpu.VMEM((end_slabs, count * chans, SPREAD_SPAN), bf16),
    ]
    own_scratch = [
        pltpu.VMEM((own_slabs * chans, rows), bf16),
        pltpu.VMEM((own_slabs, count * chans, SPREAD_SPAN), bf16),
    ]

    before = shifted(field[:, rows - HALO :], "space", 1)
    after = shifted(field[:, :HALO], "space", -1)
    grad_rows, spread_next = call(
        spread_kernel,
        [shape((chans, rows), f32), shape((chans, HALO), bf16)],
        [pltpu.VMEM((down_slabs * chans, coarse), bf16)],
        2 * kids * (rows + HALO) * chans * coarse,
        children,
        weight_down,
        grad_out,
    )
    first, slope, taken, to_next = call(
        first_kernel,
        [
            shape((chans, rows), bf16),
            shape((chans, rows), f32),
            shape((count * chans, rows), bf16),
            shape((2 * chans, HALO), bf16),
        ],
        [slabs_scratch],
        flops,
        info,
        offsets,
        weight_first,
        field,
        before,
        after,
        spread_next,
    )
    before = shifted(to_next, "space", 1)
    after = shifted(first[:, :HALO], "space", -1)
    second, d_second, grad_second, to_prev, to_next = call(
        second_kernel,
        [
            shape((chans, rows), bf16),
            shape((chans, rows), bf16),
            shape((chans, count * chans), f32),
            shape((2 * chans, HALO), bf16),
            shape((chans, HALO), bf16),
        ],
        [slabs_scratch, pltpu.VMEM((count * chans, rows), bf16)] + end_scratch,
        flops * 3 // 2,
        info,
        offsets,
        weight_second,
        first,
        before,
        after,
        field,
        grad_rows,
    )
    from_next = shifted(to_prev, "space", -1)
    from_prev = shifted(to_next, "space", 1)
    (own,) = call(
        own_kernel,
        [shape((chans, rows), f32)],
        own_scratch,
        flops // 2,
        offsets,
        weight_second,
        d_second,
    )
    coarse_out, d_first, grads = call(
        middle_kernel,
        [
            shape((coarse, wide), bf16),
            shape((chans, rows), bf16),
            shape((chans, 2 * count * chans + kids * wide), f32),
        ],
        [
            pltpu.VMEM((down_slabs * chans, DOWN_SPAN), bf16),
            pltpu.VMEM((kids * chans, coarse), bf16),
        ],
        2 * kids * (rows + HALO) * chans * coarse,
        info,
        children,
        weight_down,
        grad_out,
        second,
        from_next,
        from_prev,
        own,
        slope,
        taken,
        grad_second,
    )
    samples = lax.axis_size("dp")
    direct = samples == 4 and devices == 4
    scale = float(samples * devices * rows) ** (-0.5)
    me = lax.axis_index("dp")
    share = chans // samples

    def partner(value, step):
        return lax.ppermute(value, "dp", [(i, i ^ step) for i in range(samples)])

    def quarter(step):
        return lax.dynamic_slice_in_dim(grads, (me ^ step) * share, share, axis=0)

    if direct:
        sent = [quarter(s).astype(bf16) for s in range(1, samples)]
        got = [partner(v, s + 1) for s, v in enumerate(sent)]
    to_prev, to_next = call(
        ends_kernel,
        [shape((chans, HALO), bf16), shape((chans, HALO), bf16)],
        end_scratch,
        flops // 2,
        offsets,
        weight_first,
        d_first,
    )
    if direct:
        part = quarter(0) + sum(v.astype(f32) for v in got)
        sent = part.astype(bf16)
        got = [shifted(sent, "space", s) for s in range(1, devices)]
    after = shifted(to_prev, "space", -1)
    before = shifted(to_next, "space", 1)
    (own,) = call(
        own_kernel,
        [shape((chans, rows), f32)],
        own_scratch,
        flops // 2,
        offsets,
        weight_first,
        d_first,
    )
    if direct:
        terms = [v.astype(f32) for v in [sent] + got]
        part = (((terms[0] + terms[2]) + (terms[1] + terms[3])) * scale).astype(bf16)
        parts = [part] + [partner(part, s) for s in range(1, samples)]
        grads = jnp.zeros(grads.shape, bf16)
        for s, v in enumerate(parts):
            grads = lax.dynamic_update_slice_in_dim(grads, v, (me ^ s) * share, axis=0)
    else:
        grads = (lax.psum(grads, ("space", "dp")) * scale).astype(bf16)
    feature_grad, out_first, out_second, out_down = call(
        last_kernel,
        [
            shape((chans, rows), bf16),
            shape(weight_first.shape, bf16),
            shape(weight_second.shape, bf16),
            shape(weight_down.shape, bf16),
        ],
        [],
        1,
        info,
        own,
        d_second,
        before,
        after,
        grads,
    )
    return (coarse_out[None], feature_grad.T[None], out_first, out_second, out_down)


def solution(mesh):
    placed = (
        P(("groups", "dp"), "space", None),
        P(("groups", "dp"), None, "space"),
        P(("groups", "dp"), None, "space"),
        P(("groups", "dp"), "space"),
        P(),
        P(),
        P(),
        P(("groups", "dp"), "space", None),
    )
    return jax.shard_map(
        body,
        mesh=mesh,
        in_specs=placed,
        out_specs=(
            P(("groups", "dp"), "space", None),
            P(("groups", "dp"), "space", None),
            P("groups", None, None),
            P("groups", None, None),
            P("groups", None, None),
        ),
        check_vma=False,
    )
```

```python
import functools

import jax
import jax.numpy as jnp
from jax import lax
from jax.experimental import pallas as pl
from jax.experimental.pallas import tpu as pltpu
from jax.sharding import PartitionSpec as P

HALO = 512
READ_SPAN = 512
SPREAD_SPAN = 256
DOWN_SPAN = 512
UNROLL = 13
VMEM_BYTES = 24 * 2**20
LIVE, FIRST, LAST, DP = range(4)


def silu_slope(value):
    sig = jax.nn.sigmoid(value)
    return sig * (1.0 + value * (1.0 - sig))


def locate(index, span):
    slab = lax.shift_right_arithmetic(index, span.bit_length() - 1)
    return slab, jnp.where(index >= 0, index & (span - 1), -1)


def one_hot(place, span):
    shape = (span, place.shape[1])
    here = jnp.broadcast_to(place, shape).astype(jnp.int16)
    return jnp.where(
        here == lax.broadcasted_iota(jnp.int16, shape, 0), jnp.bfloat16(1), jnp.bfloat16(0)
    )


def nt(left, right):
    return lax.dot_general(
        left, right, (((1,), (1,)), ((), ())), preferred_element_type=jnp.float32
    )


def nn(left, right):
    return jnp.dot(left, right, preferred_element_type=jnp.float32)


def read_rows(slabs, index, chans):
    count, span = slabs.shape[0] // chans, slabs.shape[1]
    slab, place = locate(index, span)
    read = nn(slabs, one_hot(place, span))
    picked = read[(count - 1) * chans :]
    for s in range(count - 1):
        picked = jnp.where(slab == s, read[s * chans : (s + 1) * chans], picked)
    return picked.astype(jnp.bfloat16)


def spread_rows(terms_ref, terms, index, count, span):
    chans = terms.shape[0]
    slab, place = locate(index, span)
    for s in range(count):
        terms_ref[s * chans : (s + 1) * chans, :] = jnp.where(slab == s, terms, jnp.zeros_like(terms))
    return nt(terms_ref[...], one_hot(place, span))


def conv(info_ref, map_ref, weight_ref, slabs_ref, taken_ref, blocks):
    count, chans = weight_ref.shape[0], weight_ref.shape[1]
    window = map_ref.shape[2] + 2 * HALO
    centre = count // 2
    alive = live_mask(info_ref, map_ref.shape[2])
    for place, block in enumerate(blocks):
        own = slabs_ref[(block + 1) * chans : (block + 2) * chans]
        taken_ref[centre * chans : (centre + 1) * chans, place * HALO : (place + 1) * HALO] = jnp.where(
            alive[:, block * HALO : (block + 1) * HALO], own, jnp.zeros_like(own)
        )

    def step(i, carry):
        k = i + (i >= centre).astype(jnp.int32)
        index = map_ref[k]
        index = jnp.where(index < window, index, -1)
        at = pl.ds(pl.multiple_of(k * chans, chans), chans)
        for place, block in enumerate(blocks):
            part = index[:, block * HALO : (block + 1) * HALO]
            taken_ref[at, place * HALO : (place + 1) * HALO] = read_rows(slabs_ref[...], part, chans)
        return carry

    lax.fori_loop(0, count - 1, step, 0, unroll=UNROLL)
    weights = weight_ref[...].reshape(count * chans, -1).T
    return nn(weights, taken_ref[...])


def conv_back(map_ref, weight_ref, grad_ref, terms_ref, sums_ref, halo, begin, end):
    count, chans = weight_ref.shape[0], weight_ref.shape[1]
    rows = grad_ref.shape[1]
    slabs = sums_ref.shape[0]
    centre = count // 2
    holds = begin <= centre < end

    def step(i, carry):
        k = i + begin
        if holds:
            k += (k >= centre).astype(jnp.int32)
        index = map_ref[k]
        if halo:
            after = (index >= HALO + rows) & (index < 2 * HALO + rows)
            index = jnp.where(after, index - rows, jnp.where(index < HALO, index, -1))
        else:
            index = jnp.where(index < HALO + rows, index - HALO, -1)
        sums = spread_rows(terms_ref, grad_ref[...], index, slabs, SPREAD_SPAN).astype(jnp.bfloat16)
        at = pl.ds(pl.multiple_of((k - begin) * chans, chans), chans)
        for s in range(slabs):
            sums_ref[s, at, :] = sums[s * chans : (s + 1) * chans]
        return carry

    if holds:
        at = slice((centre - begin) * chans, (centre - begin + 1) * chans)
        for s in range(slabs):
            own = grad_ref[:, s * SPREAD_SPAN : (s + 1) * SPREAD_SPAN]
            sums_ref[s, at, :] = jnp.zeros_like(own) if halo else own
    lax.fori_loop(0, end - begin - holds, step, 0, unroll=UNROLL)
    weights = jnp.concatenate([weight_ref[k] for k in range(begin, end)], axis=1)
    return [nn(weights, sums_ref[s]) for s in range(slabs)]


def put_window(slabs_ref, info_ref, before, own, after):
    zero = jnp.zeros_like(before)
    before = jnp.where(info_ref[0, FIRST] == 1, zero, before)
    after = jnp.where(info_ref[0, LAST] == 1, zero, after)
    chans = before.shape[0]
    for s, part in enumerate([before] + own + [after]):
        slabs_ref[s * chans : (s + 1) * chans, :] = part


def in_parts(ref):
    return [ref[:, at : at + HALO] for at in range(0, ref.shape[1], HALO)]


def ends_around(outer_ref, inner_ref):
    first, last = in_parts(outer_ref)
    return [first] + in_parts(inner_ref) + [last]


def live_mask(info_ref, rows):
    return lax.broadcasted_iota(jnp.int32, (1, rows), 1) < info_ref[0, LIVE]


def add_ends(info_ref, rows_ref, before, after):
    rows = rows_ref.shape[1]
    before = jnp.where(info_ref[0, FIRST] == 1, 0.0, before.astype(jnp.float32))
    after = jnp.where(info_ref[0, LAST] == 1, 0.0, after.astype(jnp.float32))
    return jnp.concatenate(
        [
            rows_ref[:, :HALO] + before,
            rows_ref[:, HALO : rows - HALO],
            rows_ref[:, rows - HALO :] + after,
        ],
        axis=1,
    )


def spread_kernel(
    child_hbm, down_hbm, grad_hbm, own_ref, next_ref, terms_ref, child_ref, down_ref, grad_ref, sems
):
    copies = [
        pltpu.make_async_copy(source, target, sems.at[i])
        for i, (source, target) in enumerate(
            ((child_hbm, child_ref), (down_hbm, down_ref), (grad_hbm, grad_ref))
        )
    ]
    for copy in copies:
        copy.start()
    for copy in copies:
        copy.wait()
    kids, chans, wide = down_ref.shape
    rows = own_ref.shape[1]
    slabs = (rows + HALO) // DOWN_SPAN
    total = jnp.zeros((slabs * chans, DOWN_SPAN), jnp.float32)
    terms = nt(down_ref[...].reshape(kids * chans, wide), grad_ref[...]).astype(jnp.bfloat16)
    for j in range(kids):
        index = child_ref[j : j + 1, :]
        index = jnp.where(index < rows + HALO, index, -1)
        total += spread_rows(terms_ref, terms[j * chans : (j + 1) * chans], index, slabs, DOWN_SPAN)
    for s in range(slabs - 1):
        own_ref[:, s * DOWN_SPAN : (s + 1) * DOWN_SPAN] = total[s * chans : (s + 1) * chans]
    next_ref[...] = total[(slabs - 1) * chans :].astype(next_ref.dtype)


def first_part(info_ref, map_ref, weight_ref, slabs_ref, first_ref, slope_ref, taken_ref, blocks):
    pre = conv(info_ref, map_ref, weight_ref, slabs_ref, taken_ref, blocks)
    alive = live_mask(info_ref, map_ref.shape[2])
    for place, block in enumerate(blocks):
        part = slice(place * HALO, (place + 1) * HALO)
        lives = alive[:, block * HALO : (block + 1) * HALO]
        value = pre[:, part]
        first_ref[:, part] = jnp.where(lives, jax.nn.silu(value), 0.0).astype(jnp.bfloat16)
        slope_ref[:, part] = jnp.where(lives, silu_slope(value), 0.0)


def outer_kernel(
    info_ref,
    map_ref,
    weight_ref,
    field_ref,
    before_ref,
    after_ref,
    spread_ref,
    first_ref,
    slope_ref,
    taken_ref,
    to_next_ref,
    slabs_ref,
):
    put_window(slabs_ref, info_ref, before_ref[...], in_parts(field_ref), after_ref[...])
    blocks = [0, field_ref.shape[1] // HALO - 1]
    first_part(info_ref, map_ref, weight_ref, slabs_ref, first_ref, slope_ref, taken_ref, blocks)
    chans = field_ref.shape[0]
    to_next_ref[:chans] = first_ref[:, HALO:]
    to_next_ref[chans:] = spread_ref[...]


def inner_kernel(
    info_ref,
    map_ref,
    weight_ref,
    field_ref,
    before_ref,
    after_ref,
    first_ref,
    slope_ref,
    taken_ref,
    slabs_ref,
):
    put_window(slabs_ref, info_ref, before_ref[...], in_parts(field_ref), after_ref[...])
    blocks = list(range(1, field_ref.shape[1] // HALO - 1))
    first_part(info_ref, map_ref, weight_ref, slabs_ref, first_ref, slope_ref, taken_ref, blocks)


def second_kernel(
    info_ref,
    map_ref,
    weight_ref,
    outer_ref,
    inner_ref,
    before_ref,
    after_ref,
    field_ref,
    rows_ref,
    second_ref,
    d_second_ref,
    grad_weight_ref,
    to_prev_ref,
    to_next_ref,
    slabs_ref,
    taken_ref,
    terms_ref,
    sums_ref,
):
    chans, rows = field_ref.shape
    own = ends_around(outer_ref, inner_ref)
    put_window(slabs_ref, info_ref, before_ref[:chans], own, after_ref[...])
    blocks = list(range(rows // HALO))
    pre = conv(info_ref, map_ref, weight_ref, slabs_ref, taken_ref, blocks) + field_ref[...].astype(jnp.float32)
    alive = live_mask(info_ref, rows)
    second_ref[...] = jnp.where(alive, jax.nn.silu(pre), 0.0).astype(jnp.bfloat16)
    slope = jnp.where(alive, silu_slope(pre), 0.0)
    returned = jnp.where(info_ref[0, FIRST] == 1, 0.0, before_ref[chans:].astype(jnp.float32))
    grad_rows = jnp.concatenate([rows_ref[:, :HALO] + returned, rows_ref[:, HALO:]], axis=1)
    d_second_ref[...] = (grad_rows * slope).astype(jnp.bfloat16)
    grad_weight_ref[...] = nt(d_second_ref[...], taken_ref[...])
    ends = conv_back(map_ref, weight_ref, d_second_ref, terms_ref, sums_ref, True, 0, map_ref.shape[0])
    half = len(ends) // 2
    to_prev_ref[:chans] = jnp.concatenate(ends[:half], axis=1).astype(to_prev_ref.dtype)
    to_prev_ref[chans:] = second_ref[:, :HALO]
    to_next_ref[...] = jnp.concatenate(ends[half:], axis=1).astype(to_next_ref.dtype)


def own_kernel(begin, end, map_ref, weight_ref, grad_ref, own_ref, terms_ref, sums_ref):
    parts = conv_back(map_ref, weight_ref, grad_ref, terms_ref, sums_ref, False, begin, end)
    for s, part in enumerate(parts):
        own_ref[:, s * SPREAD_SPAN : (s + 1) * SPREAD_SPAN] = part


def ends_kernel(map_ref, weight_ref, grad_ref, to_prev_ref, to_next_ref, terms_ref, sums_ref):
    ends = conv_back(map_ref, weight_ref, grad_ref, terms_ref, sums_ref, True, 0, map_ref.shape[0])
    half = len(ends) // 2
    to_prev_ref[...] = jnp.concatenate(ends[:half], axis=1).astype(to_prev_ref.dtype)
    to_next_ref[...] = jnp.concatenate(ends[half:], axis=1).astype(to_next_ref.dtype)


def middle_kernel(
    info_ref,
    child_ref,
    down_ref,
    grad_ref,
    second_ref,
    from_next_ref,
    from_prev_ref,
    rows_ref,
    slope_outer_ref,
    slope_inner_ref,
    taken_outer_ref,
    taken_inner_ref,
    grad_second_ref,
    coarse_ref,
    d_first_ref,
    grads_ref,
    slabs_ref,
    kids_ref,
):
    kids, chans, wide = down_ref.shape
    rows = second_ref.shape[1]
    for s in range(rows // DOWN_SPAN):
        slabs_ref[s * chans : (s + 1) * chans, :] = second_ref[:, s * DOWN_SPAN : (s + 1) * DOWN_SPAN]
    after = from_next_ref[chans:]
    slabs_ref[rows // DOWN_SPAN * chans :, :] = jnp.where(
        info_ref[0, LAST] == 1, jnp.zeros_like(after), after
    )
    for j in range(kids):
        index = child_ref[j : j + 1, :]
        index = jnp.where(index < rows + HALO, index, -1)
        kids_ref[j * chans : (j + 1) * chans, :] = read_rows(slabs_ref[...], index, chans)
    taken = kids_ref[...]
    flat = down_ref[...].reshape(kids * chans, wide)
    coarse_ref[...] = nn(taken.T, flat).astype(jnp.bfloat16)
    grad_down = nn(taken, grad_ref[...])
    slope = jnp.concatenate(ends_around(slope_outer_ref, slope_inner_ref), axis=1)
    d_first = (
        add_ends(info_ref, rows_ref, from_prev_ref[...], from_next_ref[:chans]) * slope
    ).astype(jnp.bfloat16)
    d_first_ref[...] = d_first
    d_outer = jnp.concatenate([d_first[:, :HALO], d_first[:, rows - HALO :]], axis=1)
    size = grad_second_ref.shape[1]
    grads_ref[:, :size] = grad_second_ref[...]
    grads_ref[:, size : 2 * size] = nt(d_outer, taken_outer_ref[...]) + nt(
        d_first[:, HALO : rows - HALO], taken_inner_ref[...]
    )
    for j in range(kids):
        grads_ref[:, 2 * size + j * wide : 2 * size + (j + 1) * wide] = grad_down[
            j * chans : (j + 1) * chans
        ]


def last_kernel(
    info_ref,
    low_ref,
    high_ref,
    d_second_ref,
    before_ref,
    after_ref,
    grads_ref,
    field_ref,
    first_ref,
    second_ref,
    down_ref,
):
    own = low_ref[...] + high_ref[...]
    total = add_ends(info_ref, own, before_ref[...], after_ref[...])
    field_ref[...] = (total + d_second_ref[...].astype(jnp.float32)).astype(jnp.bfloat16)
    count, chans = first_ref.shape[0], first_ref.shape[1]
    kids, wide = down_ref.shape[0], down_ref.shape[2]
    size = count * chans
    second = grads_ref[:, :size].T
    first = grads_ref[:, size : 2 * size].T
    for k in range(count):
        second_ref[k] = second[k * chans : (k + 1) * chans]
        first_ref[k] = first[k * chans : (k + 1) * chans]
    for j in range(kids):
        down_ref[j] = grads_ref[:, 2 * size + j * wide : 2 * size + (j + 1) * wide]


def shape(dims, dtype):
    return jax.ShapeDtypeStruct(dims, dtype)


def call(kernel, outs, scratch, flops, *args, where=pltpu.VMEM):
    smem = pl.BlockSpec(memory_space=pltpu.SMEM)
    vmem = pl.BlockSpec(memory_space=pltpu.VMEM)
    return pl.pallas_call(
        kernel,
        out_shape=outs,
        in_specs=[smem if a.shape == (1, 4) else pl.BlockSpec(memory_space=where) for a in args],
        out_specs=[vmem] * len(outs),
        scratch_shapes=scratch,
        compiler_params=pltpu.CompilerParams(vmem_limit_bytes=VMEM_BYTES),
        cost_estimate=pl.CostEstimate(flops=flops, bytes_accessed=2**20, transcendentals=0),
    )(*args)


def shifted(value, axis, steps):
    count = lax.axis_size(axis)
    return lax.ppermute(value, axis, [(i, (i + steps) % count) for i in range(count)])


def body(
    features, kernel_map, child_map, live_rows, weight_first, weight_second, weight_down, out_grad
):
    bf16, f32 = jnp.bfloat16, jnp.float32
    field = features[0].T
    chans, rows = field.shape
    count = kernel_map.shape[1]
    offsets = kernel_map.reshape(count, 1, rows)
    children = child_map[0]
    kids, coarse = children.shape
    wide = weight_down.shape[2]
    grad_out = out_grad[0]
    place = lax.axis_index("space")
    devices = lax.axis_size("space")
    info = jnp.stack(
        [
            live_rows[0, 0],
            (place == 0).astype(jnp.int32),
            (place == devices - 1).astype(jnp.int32),
            lax.axis_index("dp").astype(jnp.int32),
        ]
    ).reshape(1, 4)
    window = rows + 2 * HALO
    flops = 2 * count * window * chans * rows
    down_slabs = (rows + HALO) // DOWN_SPAN
    end_slabs, own_slabs = 2 * HALO // SPREAD_SPAN, rows // SPREAD_SPAN
    slabs_scratch = pltpu.VMEM((window // READ_SPAN * chans, READ_SPAN), bf16)
    end_scratch = [
        pltpu.VMEM((end_slabs * chans, rows), bf16),
        pltpu.VMEM((end_slabs, count * chans, SPREAD_SPAN), bf16),
    ]

    def own_scratch(offset_count):
        return [
            pltpu.VMEM((own_slabs * chans, rows), bf16),
            pltpu.VMEM((own_slabs, offset_count * chans, SPREAD_SPAN), bf16),
        ]


    before = shifted(field[:, rows - HALO :], "space", 1)
    after = shifted(field[:, :HALO], "space", -1)
    grad_rows, spread_next = call(
        spread_kernel,
        [shape((chans, rows), f32), shape((chans, HALO), bf16)],
        [
            pltpu.VMEM((down_slabs * chans, coarse), bf16),
            pltpu.VMEM(children.shape, jnp.int32),
            pltpu.VMEM(weight_down.shape, bf16),
            pltpu.VMEM(grad_out.shape, bf16),
            pltpu.SemaphoreType.DMA((3,)),
        ],
        2 * kids * (rows + HALO) * chans * coarse,
        children,
        weight_down,
        grad_out,
        where=pltpu.HBM,
    )
    first_outer, slope_outer, taken_outer, to_next = call(
        outer_kernel,
        [
            shape((chans, 2 * HALO), bf16),
            shape((chans, 2 * HALO), f32),
            shape((count * chans, 2 * HALO), bf16),
            shape((2 * chans, HALO), bf16),
        ],
        [slabs_scratch],
        flops * 2 // 3,
        info,
        offsets,
        weight_first,
        field,
        before,
        after,
        spread_next,
    )
    before, after, first_outer, to_next = lax.optimization_barrier((before, after, first_outer, to_next))
    first_inner, slope_inner, taken_inner = call(
        inner_kernel,
        [
            shape((chans, rows - 2 * HALO), bf16),
            shape((chans, rows - 2 * HALO), f32),
            shape((count * chans, rows - 2 * HALO), bf16),
        ],
        [slabs_scratch],
        flops // 3,
        info,
        offsets,
        weight_first,
        field,
        before,
        after,
    )
    before = shifted(to_next, "space", 1)
    after = shifted(first_outer[:, :HALO], "space", -1)
    second, d_second, grad_second, to_prev, to_next = call(
        second_kernel,
        [
            shape((chans, rows), bf16),
            shape((chans, rows), bf16),
            shape((chans, count * chans), f32),
            shape((2 * chans, HALO), bf16),
            shape((chans, HALO), bf16),
        ],
        [slabs_scratch, pltpu.VMEM((count * chans, rows), bf16)] + end_scratch,
        flops * 3 // 2,
        info,
        offsets,
        weight_second,
        first_outer,
        first_inner,
        before,
        after,
        field,
        grad_rows,
    )
    from_next = shifted(to_prev, "space", -1)
    from_prev = shifted(to_next, "space", 1)
    (own,) = call(
        functools.partial(own_kernel, 0, count),
        [shape((chans, rows), f32)],
        own_scratch(count),
        flops // 2,
        offsets,
        weight_second,
        d_second,
    )
    coarse_out, d_first, grads = call(
        middle_kernel,
        [
            shape((coarse, wide), bf16),
            shape((chans, rows), bf16),
            shape((chans, 2 * count * chans + kids * wide), f32),
        ],
        [
            pltpu.VMEM((down_slabs * chans, DOWN_SPAN), bf16),
            pltpu.VMEM((kids * chans, coarse), bf16),
        ],
        2 * kids * (rows + HALO) * chans * coarse,
        info,
        children,
        weight_down,
        grad_out,
        second,
        from_next,
        from_prev,
        own,
        slope_outer,
        slope_inner,
        taken_outer,
        taken_inner,
        grad_second,
    )
    samples = lax.axis_size("dp")
    direct = samples == 4 and devices == 4
    scale = float(samples * devices * rows) ** (-0.5)
    me = lax.axis_index("dp")
    share = chans // samples

    def partner(value, step):
        return lax.ppermute(value, "dp", [(i, i ^ step) for i in range(samples)])

    def quarter(step):
        return lax.dynamic_slice_in_dim(grads, (me ^ step) * share, share, axis=0)

    def own_half(begin, end, grad):
        (half,) = call(
            functools.partial(own_kernel, begin, end),
            [shape((chans, rows), f32)],
            own_scratch(end - begin),
            flops // 4,
            offsets,
            weight_first,
            grad,
        )
        return half

    if direct:
        sent = [quarter(s).astype(bf16) for s in range(1, samples)]
        sent, d_first = lax.optimization_barrier((sent, d_first))
        got = [partner(v, s + 1) for s, v in enumerate(sent)]
    to_prev, to_next = call(
        ends_kernel,
        [shape((chans, HALO), bf16), shape((chans, HALO), bf16)],
        end_scratch,
        flops // 2,
        offsets,
        weight_first,
        d_first,
    )
    if direct:
        got, to_prev, to_next = lax.optimization_barrier((got, to_prev, to_next))
        sent = (quarter(0) + sum(v.astype(f32) for v in got)).astype(bf16)
        sent, d_first = lax.optimization_barrier((sent, d_first))
        got = [shifted(sent, "space", s) for s in range(1, devices)]
    after = shifted(to_prev, "space", -1)
    before = shifted(to_next, "space", 1)
    low = own_half(0, count // 2, d_first)
    if direct:
        got, low = lax.optimization_barrier((got, low))
        terms = [v.astype(f32) for v in [sent] + got]
        part = (((terms[0] + terms[2]) + (terms[1] + terms[3])) * scale).astype(bf16)
        part, d_first = lax.optimization_barrier((part, d_first))
        parts = [part] + [partner(part, s) for s in range(1, samples)]
    high = own_half(count // 2, count, d_first)
    if direct:
        parts, high = lax.optimization_barrier((parts, high))
        grads = jnp.zeros(grads.shape, bf16)
        for s, v in enumerate(parts):
            grads = lax.dynamic_update_slice_in_dim(grads, v, (me ^ s) * share, axis=0)
    else:
        grads = (lax.psum(grads, ("space", "dp")) * scale).astype(bf16)
    feature_grad, out_first, out_second, out_down = call(
        last_kernel,
        [
            shape((chans, rows), bf16),
            shape(weight_first.shape, bf16),
            shape(weight_second.shape, bf16),
            shape(weight_down.shape, bf16),
        ],
        [],
        1,
        info,
        low,
        high,
        d_second,
        before,
        after,
        grads,
    )
    return (coarse_out[None], feature_grad.T[None], out_first, out_second, out_down)


def solution(mesh):
    placed = (
        P(("groups", "dp"), "space", None),
        P(("groups", "dp"), None, "space"),
        P(("groups", "dp"), None, "space"),
        P(("groups", "dp"), "space"),
        P(),
        P(),
        P(),
        P(("groups", "dp"), "space", None),
    )
    return jax.shard_map(
        body,
        mesh=mesh,
        in_specs=placed,
        out_specs=(
            P(("groups", "dp"), "space", None),
            P(("groups", "dp"), "space", None),
            P("groups", None, None),
            P("groups", None, None),
            P("groups", None, None),
        ),
        check_vma=False,
    )
```

```python
import functools

import jax
import jax.numpy as jnp
from jax import lax
from jax.experimental import pallas as pl
from jax.experimental.pallas import tpu as pltpu
from jax.sharding import PartitionSpec as P

HALO = 512
READ_SLABS = 2
SPREAD_SPAN = 256
DOWN_SPAN = 512
LOW = 18
ROW = 16
UNROLL = 8
VMEM_BYTES = 24 * 2**20
LIVE, FIRST, LAST, DP = range(4)


def silu_slope(value):
    sig = jax.nn.sigmoid(value)
    return sig * (1.0 + value * (1.0 - sig))


def locate(index, span, count):
    slab = sum((index >= span * s).astype(jnp.int32) for s in range(1, count))
    return slab, jnp.where(index >= 0, index - slab * span, -1)


def one_hot(place, span):
    shape = (span, place.shape[1])
    here = jnp.broadcast_to(place, shape).astype(jnp.int16)
    return jnp.where(
        here == lax.broadcasted_iota(jnp.int16, shape, 0), jnp.bfloat16(1), jnp.bfloat16(0)
    )


def nt(left, right):
    return lax.dot_general(
        left, right, (((1,), (1,)), ((), ())), preferred_element_type=jnp.float32
    )


def nn(left, right):
    return jnp.dot(left, right, preferred_element_type=jnp.float32)


def repeat(step, count):
    rounds, rest = divmod(count, min(UNROLL, max(1, count // 2)))
    steps = (count - rest) // rounds

    def turn(i, carry):
        for u in range(steps):
            step(i * steps + u)
        return carry

    lax.fori_loop(0, rounds, turn, 0)
    for u in range(count - rest, count):
        step(jnp.int32(u))


def read_rows(slabs, index, chans):
    count, span = slabs.shape[0] // chans, slabs.shape[1]
    slab, place = locate(index, span, count)
    read = nn(slabs, one_hot(place, span))
    picked = read[(count - 1) * chans :]
    for s in range(count - 1):
        picked = jnp.where(slab == s, read[s * chans : (s + 1) * chans], picked)
    return picked.astype(jnp.bfloat16)


def spread_rows(terms_ref, terms, index, count, span):
    chans = terms.shape[0]
    slab, place = locate(index, span, count)
    for s in range(count):
        terms_ref[s * chans : (s + 1) * chans, :] = jnp.where(slab == s, terms, jnp.zeros_like(terms))
    return nt(terms_ref[...], one_hot(place, span))


def conv(info_ref, map_ref, weight_ref, slabs_ref, taken_ref, own, blocks):
    count, chans = weight_ref.shape[0], weight_ref.shape[1]
    window = map_ref.shape[2] + 2 * HALO
    centre = count // 2
    alive = live_mask(info_ref, map_ref.shape[2])
    for place, block in enumerate(blocks):
        taken_ref[centre * chans : (centre + 1) * chans, place * HALO : (place + 1) * HALO] = jnp.where(
            alive[:, block * HALO : (block + 1) * HALO], own[block], jnp.zeros_like(own[block])
        )

    def step(i):
        k = i + (i >= centre).astype(jnp.int32)
        index = map_ref[k]
        index = jnp.where(index < window, index, -1)
        at = pl.ds(pl.multiple_of(k * chans, chans), chans)
        for place, block in enumerate(blocks):
            part = index[:, block * HALO : (block + 1) * HALO]
            taken_ref[at, place * HALO : (place + 1) * HALO] = read_rows(slabs_ref[...], part, chans)

    repeat(step, count - 1)
    weights = weight_ref[...].reshape(count * chans, -1).T
    return nn(weights, taken_ref[...])


def conv_back(map_ref, weight_ref, grad_ref, terms_ref, sums_ref, halo, begin, end):
    count, chans = weight_ref.shape[0], weight_ref.shape[1]
    rows = grad_ref.shape[1]
    slabs = sums_ref.shape[0]
    centre = count // 2
    holds = begin <= centre < end

    def step(i):
        k = i + begin
        if holds:
            k += (k >= centre).astype(jnp.int32)
        index = map_ref[k]
        if halo:
            after = (index >= HALO + rows) & (index < 2 * HALO + rows)
            index = jnp.where(after, index - rows, jnp.where(index < HALO, index, -1))
        else:
            index = jnp.where(index < HALO + rows, index - HALO, -1)
        sums = spread_rows(terms_ref, grad_ref[...], index, slabs, SPREAD_SPAN).astype(jnp.bfloat16)
        at = pl.ds(pl.multiple_of((k - begin) * chans, chans), chans)
        for s in range(slabs):
            sums_ref[s, at, :] = sums[s * chans : (s + 1) * chans]

    if holds:
        at = slice((centre - begin) * chans, (centre - begin + 1) * chans)
        for s in range(slabs):
            own = grad_ref[:, s * SPREAD_SPAN : (s + 1) * SPREAD_SPAN]
            sums_ref[s, at, :] = jnp.zeros_like(own) if halo else own
    repeat(step, end - begin - holds)
    weights = jnp.concatenate([weight_ref[k] for k in range(begin, end)], axis=1)
    return [nn(weights, sums_ref[s]) for s in range(slabs)]


def put_window(slabs_ref, info_ref, before, own, after):
    zero = jnp.zeros_like(before)
    before = jnp.where(info_ref[0, FIRST] == 1, zero, before)
    after = jnp.where(info_ref[0, LAST] == 1, zero, after)
    chans, span = before.shape[0], slabs_ref.shape[1]
    at = 0
    for part in [before] + own + [after]:
        done = 0
        while done < part.shape[1]:
            slab, column = divmod(at, span)
            take = min(span - column, part.shape[1] - done)
            slabs_ref[slab * chans : (slab + 1) * chans, column : column + take] = part[
                :, done : done + take
            ]
            done, at = done + take, at + take


def in_parts(ref):
    return [ref[:, at : at + HALO] for at in range(0, ref.shape[1], HALO)]


def ends_around(outer_ref, inner_ref):
    first, last = in_parts(outer_ref)
    return [first] + in_parts(inner_ref) + [last]


def live_mask(info_ref, rows):
    return lax.broadcasted_iota(jnp.int32, (1, rows), 1) < info_ref[0, LIVE]


def add_ends(info_ref, own, before, after):
    rows = own.shape[1]
    before = jnp.where(info_ref[0, FIRST] == 1, 0.0, before.astype(jnp.float32))
    after = jnp.where(info_ref[0, LAST] == 1, 0.0, after.astype(jnp.float32))
    return jnp.concatenate(
        [
            own[:, :HALO] + before,
            own[:, HALO : rows - HALO],
            own[:, rows - HALO :] + after,
        ],
        axis=1,
    )


def spread_kernel(
    child_hbm, down_hbm, grad_hbm, own_ref, next_ref, terms_ref, child_ref, down_ref, grad_ref, sems
):
    copies = [
        pltpu.make_async_copy(source, target, sems.at[i])
        for i, (source, target) in enumerate(
            ((child_hbm, child_ref), (down_hbm, down_ref), (grad_hbm, grad_ref))
        )
    ]
    for copy in copies:
        copy.start()
    for copy in copies:
        copy.wait()
    kids, chans, wide = down_ref.shape
    rows = own_ref.shape[1]
    slabs = (rows + HALO) // DOWN_SPAN
    total = jnp.zeros((slabs * chans, DOWN_SPAN), jnp.float32)
    terms = nt(down_ref[...].reshape(kids * chans, wide), grad_ref[...]).astype(jnp.bfloat16)
    for j in range(kids):
        index = child_ref[j : j + 1, :]
        index = jnp.where(index < rows + HALO, index, -1)
        total += spread_rows(terms_ref, terms[j * chans : (j + 1) * chans], index, slabs, DOWN_SPAN)
    for s in range(slabs - 1):
        own_ref[:, s * DOWN_SPAN : (s + 1) * DOWN_SPAN] = total[s * chans : (s + 1) * chans]
    next_ref[...] = total[(slabs - 1) * chans :].astype(next_ref.dtype)


def first_part(info_ref, map_ref, weight_ref, field_ref, slabs_ref, first_ref, slope_ref, taken_ref, blocks):
    pre = conv(info_ref, map_ref, weight_ref, slabs_ref, taken_ref, in_parts(field_ref), blocks)
    alive = live_mask(info_ref, map_ref.shape[2])
    for place, block in enumerate(blocks):
        part = slice(place * HALO, (place + 1) * HALO)
        lives = alive[:, block * HALO : (block + 1) * HALO]
        value = pre[:, part]
        first_ref[:, part] = jnp.where(lives, jax.nn.silu(value), 0.0).astype(jnp.bfloat16)
        slope_ref[:, part] = jnp.where(lives, silu_slope(value), 0.0)


def outer_kernel(
    info_ref,
    map_ref,
    weight_ref,
    field_ref,
    before_ref,
    after_ref,
    spread_ref,
    first_ref,
    slope_ref,
    taken_ref,
    to_next_ref,
    slabs_ref,
):
    put_window(slabs_ref, info_ref, before_ref[...], in_parts(field_ref), after_ref[...])
    blocks = [0, field_ref.shape[1] // HALO - 1]
    first_part(
        info_ref, map_ref, weight_ref, field_ref, slabs_ref, first_ref, slope_ref, taken_ref, blocks
    )
    chans = field_ref.shape[0]
    to_next_ref[:chans] = first_ref[:, HALO:]
    to_next_ref[chans:] = spread_ref[...]


def inner_kernel(
    info_ref,
    map_ref,
    weight_ref,
    field_ref,
    before_ref,
    after_ref,
    first_ref,
    slope_ref,
    taken_ref,
    slabs_ref,
):
    put_window(slabs_ref, info_ref, before_ref[...], in_parts(field_ref), after_ref[...])
    blocks = list(range(1, field_ref.shape[1] // HALO - 1))
    first_part(
        info_ref, map_ref, weight_ref, field_ref, slabs_ref, first_ref, slope_ref, taken_ref, blocks
    )


def second_kernel(
    info_ref,
    map_ref,
    weight_ref,
    outer_ref,
    inner_ref,
    before_ref,
    after_ref,
    field_ref,
    rows_ref,
    second_ref,
    d_second_ref,
    grad_weight_ref,
    to_prev_ref,
    to_next_ref,
    slabs_ref,
    taken_ref,
    terms_ref,
    sums_ref,
):
    chans, rows = field_ref.shape
    own = ends_around(outer_ref, inner_ref)
    put_window(slabs_ref, info_ref, before_ref[:chans], own, after_ref[...])
    blocks = list(range(rows // HALO))
    pre = conv(info_ref, map_ref, weight_ref, slabs_ref, taken_ref, own, blocks) + field_ref[...].astype(jnp.float32)
    alive = live_mask(info_ref, rows)
    second_ref[...] = jnp.where(alive, jax.nn.silu(pre), 0.0).astype(jnp.bfloat16)
    slope = jnp.where(alive, silu_slope(pre), 0.0)
    returned = jnp.where(info_ref[0, FIRST] == 1, 0.0, before_ref[chans:].astype(jnp.float32))
    grad_rows = jnp.concatenate([rows_ref[:, :HALO] + returned, rows_ref[:, HALO:]], axis=1)
    d_second_ref[...] = (grad_rows * slope).astype(jnp.bfloat16)
    grad_weight_ref[...] = nt(d_second_ref[...], taken_ref[...])
    ends = conv_back(
        map_ref, weight_ref, d_second_ref, terms_ref, sums_ref, True, 0, map_ref.shape[0]
    )
    half = len(ends) // 2
    to_prev_ref[:chans] = jnp.concatenate(ends[:half], axis=1).astype(to_prev_ref.dtype)
    to_prev_ref[chans:] = second_ref[:, :HALO]
    to_next_ref[...] = jnp.concatenate(ends[half:], axis=1).astype(to_next_ref.dtype)


def own_kernel(begin, end, map_ref, weight_ref, grad_ref, own_ref, terms_ref, sums_ref):
    parts = conv_back(map_ref, weight_ref, grad_ref, terms_ref, sums_ref, False, begin, end)
    for s, part in enumerate(parts):
        own_ref[:, s * SPREAD_SPAN : (s + 1) * SPREAD_SPAN] = part


def low_kernel(
    begin, end, map_ref, weight_ref, grad_ref, kids_ref, down_ref, own_ref, coarse_ref, terms_ref, sums_ref
):
    own_kernel(begin, end, map_ref, weight_ref, grad_ref, own_ref, terms_ref, sums_ref)
    kids, chans, wide = down_ref.shape
    flat = down_ref[...].reshape(kids * chans, wide)
    coarse_ref[...] = nn(kids_ref[...].T, flat).astype(jnp.bfloat16)


def ends_kernel(map_ref, weight_ref, grad_ref, to_prev_ref, to_next_ref, terms_ref, sums_ref):
    ends = conv_back(map_ref, weight_ref, grad_ref, terms_ref, sums_ref, True, 0, map_ref.shape[0])
    half = len(ends) // 2
    for ref, parts in ((to_prev_ref, ends[:half]), (to_next_ref, ends[half:])):
        stack_to_row(ref, jnp.concatenate(parts, axis=1).astype(ref.dtype))


def stack_to_row(ref, value):
    group, width = ref.shape[0], value.shape[1]
    for i in range(value.shape[0] // group):
        ref[:, i * width : (i + 1) * width] = value[i * group : (i + 1) * group]


def row_to_stack(ref, chans):
    width = ref.shape[1] * ref.shape[0] // chans
    return jnp.concatenate([ref[:, i : i + width] for i in range(0, ref.shape[1], width)], axis=0)


def middle_kernel(
    info_ref,
    child_ref,
    down_ref,
    grad_ref,
    second_ref,
    from_next_ref,
    from_prev_ref,
    rows_ref,
    slope_outer_ref,
    slope_inner_ref,
    taken_outer_ref,
    taken_inner_ref,
    grad_second_ref,
    d_first_ref,
    grads_ref,
    kids_ref,
    slabs_ref,
):
    kids, chans, wide = down_ref.shape
    rows = second_ref.shape[1]
    for s in range(rows // DOWN_SPAN):
        slabs_ref[s * chans : (s + 1) * chans, :] = second_ref[:, s * DOWN_SPAN : (s + 1) * DOWN_SPAN]
    after = from_next_ref[chans:]
    slabs_ref[rows // DOWN_SPAN * chans :, :] = jnp.where(
        info_ref[0, LAST] == 1, jnp.zeros_like(after), after
    )
    for j in range(kids):
        index = child_ref[j : j + 1, :]
        index = jnp.where(index < rows + HALO, index, -1)
        kids_ref[j * chans : (j + 1) * chans, :] = read_rows(slabs_ref[...], index, chans)
    grad_down = nn(kids_ref[...], grad_ref[...])
    slope = jnp.concatenate(ends_around(slope_outer_ref, slope_inner_ref), axis=1)
    d_first = (
        add_ends(info_ref, rows_ref[...], from_prev_ref[...], from_next_ref[:chans]) * slope
    ).astype(jnp.bfloat16)
    d_first_ref[...] = d_first
    d_outer = jnp.concatenate([d_first[:, :HALO], d_first[:, rows - HALO :]], axis=1)
    size = grad_second_ref.shape[1]
    grads_ref[:, :size] = grad_second_ref[...]
    grads_ref[:, size : 2 * size] = nt(d_outer, taken_outer_ref[...]) + nt(
        d_first[:, HALO : rows - HALO], taken_inner_ref[...]
    )
    for j in range(kids):
        grads_ref[:, 2 * size + j * wide : 2 * size + (j + 1) * wide] = grad_down[
            j * chans : (j + 1) * chans
        ]


def last_kernel(info_ref, low_ref, high_ref, d_second_ref, before_ref, after_ref, *refs):
    quarters, (field_ref, first_ref, second_ref, down_ref, grads_ref) = refs[:-5], refs[-5:]
    chans = low_ref.shape[0]
    before, after = row_to_stack(before_ref, chans), row_to_stack(after_ref, chans)
    total = add_ends(info_ref, low_ref[...] + high_ref[...], before, after)
    field_ref[...] = (total + d_second_ref[...].astype(jnp.float32)).astype(jnp.bfloat16)
    share = quarters[0].shape[0]
    for step, quarter_ref in enumerate(quarters):
        at = (info_ref[0, DP] ^ step) * share if len(quarters) > 1 else 0
        grads_ref[pl.ds(pl.multiple_of(at, ROW), share), :] = quarter_ref[...]
    count = first_ref.shape[0]
    kids, wide = down_ref.shape[0], down_ref.shape[2]
    size = count * chans
    second = grads_ref[:, :size].T
    first = grads_ref[:, size : 2 * size].T
    for k in range(count):
        second_ref[k] = second[k * chans : (k + 1) * chans]
        first_ref[k] = first[k * chans : (k + 1) * chans]
    for j in range(kids):
        down_ref[j] = grads_ref[:, 2 * size + j * wide : 2 * size + (j + 1) * wide]


def shape(dims, dtype):
    return jax.ShapeDtypeStruct(dims, dtype)


def call(kernel, outs, scratch, flops, *args, where=pltpu.VMEM, limit=VMEM_BYTES):
    smem = pl.BlockSpec(memory_space=pltpu.SMEM)
    vmem = pl.BlockSpec(memory_space=pltpu.VMEM)
    return pl.pallas_call(
        kernel,
        out_shape=outs,
        in_specs=[smem if a.shape == (1, 4) else pl.BlockSpec(memory_space=where) for a in args],
        out_specs=[vmem] * len(outs),
        scratch_shapes=scratch,
        compiler_params=pltpu.CompilerParams(vmem_limit_bytes=limit),
        cost_estimate=pl.CostEstimate(flops=flops, bytes_accessed=2**20, transcendentals=0),
    )(*args)


def shifted(value, axis, steps):
    count = lax.axis_size(axis)
    return lax.ppermute(value, axis, [(i, (i + steps) % count) for i in range(count)])


def body(
    features, kernel_map, child_map, live_rows, weight_first, weight_second, weight_down, out_grad
):
    bf16, f32 = jnp.bfloat16, jnp.float32
    field = features[0].T
    chans, rows = field.shape
    count = kernel_map.shape[1]
    offsets = kernel_map.reshape(count, 1, rows)
    children = child_map[0]
    kids, coarse = children.shape
    wide = weight_down.shape[2]
    grad_out = out_grad[0]
    place = lax.axis_index("space")
    devices = lax.axis_size("space")
    info = jnp.stack(
        [
            live_rows[0, 0],
            (place == 0).astype(jnp.int32),
            (place == devices - 1).astype(jnp.int32),
            lax.axis_index("dp").astype(jnp.int32),
        ]
    ).reshape(1, 4)
    window = rows + 2 * HALO
    flops = 2 * count * window * chans * rows
    down_slabs = (rows + HALO) // DOWN_SPAN
    slabs_scratch = pltpu.VMEM((READ_SLABS * chans, window // READ_SLABS), bf16)

    def back_scratch(width, offset_count):
        slabs = width // SPREAD_SPAN
        return [
            pltpu.VMEM((slabs * chans, rows), bf16),
            pltpu.VMEM((slabs, offset_count * chans, SPREAD_SPAN), bf16),
        ]

    before = shifted(field[:, rows - HALO :], "space", 1)
    after = shifted(field[:, :HALO], "space", -1)
    grad_rows, spread_next = call(
        spread_kernel,
        [shape((chans, rows), f32), shape((chans, HALO), bf16)],
        [
            pltpu.VMEM((down_slabs * chans, coarse), bf16),
            pltpu.VMEM(children.shape, jnp.int32),
            pltpu.VMEM(weight_down.shape, bf16),
            pltpu.VMEM(grad_out.shape, bf16),
            pltpu.SemaphoreType.DMA((3,)),
        ],
        2 * kids * (rows + HALO) * chans * coarse,
        children,
        weight_down,
        grad_out,
        where=pltpu.HBM,
        limit=60 * 2**20,
    )
    first_outer, slope_outer, taken_outer, to_next = call(
        outer_kernel,
        [
            shape((chans, 2 * HALO), bf16),
            shape((chans, 2 * HALO), f32),
            shape((count * chans, 2 * HALO), bf16),
            shape((2 * chans, HALO), bf16),
        ],
        [slabs_scratch],
        flops * 2 // 3,
        info,
        offsets,
        weight_first,
        field,
        before,
        after,
        spread_next,
    )
    before, after, first_outer, to_next = lax.optimization_barrier((before, after, first_outer, to_next))
    first_inner, slope_inner, taken_inner = call(
        inner_kernel,
        [
            shape((chans, rows - 2 * HALO), bf16),
            shape((chans, rows - 2 * HALO), f32),
            shape((count * chans, rows - 2 * HALO), bf16),
        ],
        [slabs_scratch],
        flops // 3,
        info,
        offsets,
        weight_first,
        field,
        before,
        after,
    )
    before = shifted(to_next, "space", 1)
    after = shifted(first_outer[:, :HALO], "space", -1)
    second, d_second, grad_second, to_prev, to_next = call(
        second_kernel,
        [
            shape((chans, rows), bf16),
            shape((chans, rows), bf16),
            shape((chans, count * chans), f32),
            shape((2 * chans, HALO), bf16),
            shape((chans, HALO), bf16),
        ],
        [slabs_scratch, pltpu.VMEM((count * chans, rows), bf16)]
        + back_scratch(2 * HALO, count),
        flops * 3 // 2,
        info,
        offsets,
        weight_second,
        first_outer,
        first_inner,
        before,
        after,
        field,
        grad_rows,
    )
    from_next = shifted(to_prev, "space", -1)
    from_prev = shifted(to_next, "space", 1)
    (own,) = call(
        functools.partial(own_kernel, 0, count),
        [shape((chans, rows), f32)],
        back_scratch(rows, count),
        flops // 2,
        offsets,
        weight_second,
        d_second,
    )
    d_first, grads, kid_rows = call(
        middle_kernel,
        [
            shape((chans, rows), bf16),
            shape((chans, 2 * count * chans + kids * wide), f32),
            shape((kids * chans, coarse), bf16),
        ],
        [pltpu.VMEM((down_slabs * chans, DOWN_SPAN), bf16)],
        2 * kids * (rows + HALO) * chans * coarse,
        info,
        children,
        weight_down,
        grad_out,
        second,
        from_next,
        from_prev,
        own,
        slope_outer,
        slope_inner,
        taken_outer,
        taken_inner,
        grad_second,
    )
    samples = lax.axis_size("dp")
    direct = samples == 4 and devices == 4 and chans // samples == ROW
    scale = float(samples * devices * rows) ** (-0.5)
    me = lax.axis_index("dp")
    share = chans // samples

    def partner(value, step):
        return lax.ppermute(value, "dp", [(i, i ^ step) for i in range(samples)])

    def quarter(step):
        return lax.dynamic_slice_in_dim(grads, (me ^ step) * share, share, axis=0)

    if direct:
        sent = [quarter(s).astype(bf16) for s in range(1, samples)]
        sent, d_first = lax.optimization_barrier((sent, d_first))
        got = [partner(v, s + 1) for s, v in enumerate(sent)]
    to_prev, to_next = call(
        ends_kernel,
        [shape((ROW, chans // ROW * HALO), bf16), shape((ROW, chans // ROW * HALO), bf16)],
        back_scratch(2 * HALO, count),
        flops // 2,
        offsets,
        weight_first,
        d_first,
    )
    if direct:
        got, to_prev, to_next = lax.optimization_barrier((got, to_prev, to_next))
        sent = (quarter(0) + sum(v.astype(f32) for v in got)).astype(bf16)
        sent, d_first = lax.optimization_barrier((sent, d_first))
        forth = shifted(jnp.concatenate([sent, to_next], axis=1), "space", 1)
        back = shifted(jnp.concatenate([sent, to_prev], axis=1), "space", -1)
        across = shifted(sent, "space", 2)
    else:
        after = shifted(to_prev, "space", -1)
        before = shifted(to_next, "space", 1)
    low, coarse_out = call(
        functools.partial(low_kernel, 0, LOW),
        [shape((chans, rows), f32), shape((coarse, wide), bf16)],
        back_scratch(rows, LOW),
        flops // 3,
        offsets,
        weight_first,
        d_first,
        kid_rows,
        weight_down,
    )
    if direct:
        forth, back, across, low = lax.optimization_barrier((forth, back, across, low))
        width = grads.shape[1]
        before, after = forth[:, width:], back[:, width:]
        even = sent.astype(f32) + across.astype(f32)
        odd = forth[:, :width].astype(f32) + back[:, :width].astype(f32)
        part = ((even + odd) * scale).astype(bf16)
        part, d_first = lax.optimization_barrier((part, d_first))
        parts = [part, partner(part, 1), partner(part, 2)]
    (high,) = call(
        functools.partial(own_kernel, LOW, count),
        [shape((chans, rows), f32)],
        back_scratch(rows, count - LOW),
        flops // 6,
        offsets,
        weight_first,
        d_first,
    )
    if direct:
        parts, high = lax.optimization_barrier((parts, high))
        parts.append(partner(parts[2], 1))
    else:
        parts = [(lax.psum(grads, ("space", "dp")) * scale).astype(bf16)]
    feature_grad, out_first, out_second, out_down = call(
        last_kernel,
        [
            shape((chans, rows), bf16),
            shape(weight_first.shape, bf16),
            shape(weight_second.shape, bf16),
            shape(weight_down.shape, bf16),
        ],
        [pltpu.VMEM(grads.shape, bf16)],
        1,
        info,
        low,
        high,
        d_second,
        before,
        after,
        *parts,
    )
    return (coarse_out[None], feature_grad.T[None], out_first, out_second, out_down)


def solution(mesh):
    placed = (
        P(("groups", "dp"), "space", None),
        P(("groups", "dp"), None, "space"),
        P(("groups", "dp"), None, "space"),
        P(("groups", "dp"), "space"),
        P(),
        P(),
        P(),
        P(("groups", "dp"), "space", None),
    )
    return jax.shard_map(
        body,
        mesh=mesh,
        in_specs=placed,
        out_specs=(
            P(("groups", "dp"), "space", None),
            P(("groups", "dp"), "space", None),
            P("groups", None, None),
            P("groups", None, None),
            P("groups", None, None),
        ),
        check_vma=False,
    )
```

```python
import functools

import jax
import jax.numpy as jnp
from jax import lax
from jax.experimental import pallas as pl
from jax.experimental.pallas import tpu as pltpu
from jax.sharding import PartitionSpec as P

HALO = 512
READ_SLABS = 2
SPREAD_SPAN = 256
DOWN_SPAN = 512
LOW = 18
ROW = 16
UNROLL = 8
VMEM_BYTES = 24 * 2**20
LIVE, FIRST, LAST, DP = range(4)


def silu_slope(value):
    sig = jax.nn.sigmoid(value)
    return sig * (1.0 + value * (1.0 - sig))


def locate(index, span, count):
    slab = sum((index >= span * s).astype(jnp.int32) for s in range(1, count))
    return slab, jnp.where(index >= 0, index - slab * span, -1)


def one_hot(place, span):
    shape = (span, place.shape[1])
    here = jnp.broadcast_to(place, shape).astype(jnp.int16)
    return jnp.where(
        here == lax.broadcasted_iota(jnp.int16, shape, 0), jnp.bfloat16(1), jnp.bfloat16(0)
    )


def nt(left, right):
    return lax.dot_general(
        left, right, (((1,), (1,)), ((), ())), preferred_element_type=jnp.float32
    )


def nn(left, right):
    return jnp.dot(left, right, preferred_element_type=jnp.float32)


def repeat(step, count):
    rounds, rest = divmod(count, min(UNROLL, max(1, count // 2)))
    steps = (count - rest) // rounds

    def turn(i, carry):
        for u in range(steps):
            step(i * steps + u)
        return carry

    lax.fori_loop(0, rounds, turn, 0)
    for u in range(count - rest, count):
        step(jnp.int32(u))


def read_rows(slabs, index, chans):
    count, span = slabs.shape[0] // chans, slabs.shape[1]
    slab, place = locate(index, span, count)
    read = nn(slabs, one_hot(place, span))
    picked = read[(count - 1) * chans :]
    for s in range(count - 1):
        picked = jnp.where(slab == s, read[s * chans : (s + 1) * chans], picked)
    return picked.astype(jnp.bfloat16)


def spread_rows(terms_ref, terms, index, count, span):
    chans = terms.shape[0]
    slab, place = locate(index, span, count)
    for s in range(count):
        terms_ref[s * chans : (s + 1) * chans, :] = jnp.where(slab == s, terms, jnp.zeros_like(terms))
    return nt(terms_ref[...], one_hot(place, span))


def conv(info_ref, map_ref, weight_ref, slabs_ref, taken_ref, own, blocks):
    count, chans = weight_ref.shape[0], weight_ref.shape[1]
    window = map_ref.shape[2] + 2 * HALO
    centre = count // 2
    alive = live_mask(info_ref, map_ref.shape[2])
    for place, block in enumerate(blocks):
        taken_ref[centre * chans : (centre + 1) * chans, place * HALO : (place + 1) * HALO] = jnp.where(
            alive[:, block * HALO : (block + 1) * HALO], own[block], jnp.zeros_like(own[block])
        )

    def step(i):
        k = i + (i >= centre).astype(jnp.int32)
        index = map_ref[k]
        index = jnp.where(index < window, index, -1)
        at = pl.ds(pl.multiple_of(k * chans, chans), chans)
        for place, block in enumerate(blocks):
            part = index[:, block * HALO : (block + 1) * HALO]
            taken_ref[at, place * HALO : (place + 1) * HALO] = read_rows(slabs_ref[...], part, chans)

    repeat(step, count - 1)
    weights = weight_ref[...].reshape(count * chans, -1).T
    return nn(weights, taken_ref[...])


def conv_back(map_ref, weight_ref, grad_ref, terms_ref, sums_ref, halo, begin, end):
    count, chans = weight_ref.shape[0], weight_ref.shape[1]
    rows = grad_ref.shape[1]
    slabs = sums_ref.shape[0]
    centre = count // 2
    holds = begin <= centre < end

    def step(i):
        k = i + begin
        if holds:
            k += (k >= centre).astype(jnp.int32)
        index = map_ref[k]
        if halo:
            after = (index >= HALO + rows) & (index < 2 * HALO + rows)
            index = jnp.where(after, index - rows, jnp.where(index < HALO, index, -1))
        else:
            index = jnp.where(index < HALO + rows, index - HALO, -1)
        sums = spread_rows(terms_ref, grad_ref[...], index, slabs, SPREAD_SPAN).astype(jnp.bfloat16)
        at = pl.ds(pl.multiple_of((k - begin) * chans, chans), chans)
        for s in range(slabs):
            sums_ref[s, at, :] = sums[s * chans : (s + 1) * chans]

    if holds:
        at = slice((centre - begin) * chans, (centre - begin + 1) * chans)
        for s in range(slabs):
            own = grad_ref[:, s * SPREAD_SPAN : (s + 1) * SPREAD_SPAN]
            sums_ref[s, at, :] = jnp.zeros_like(own) if halo else own
    repeat(step, end - begin - holds)
    weights = jnp.concatenate([weight_ref[k] for k in range(begin, end)], axis=1)
    return [nn(weights, sums_ref[s]) for s in range(slabs)]


def put_window(slabs_ref, info_ref, before, own, after):
    zero = jnp.zeros_like(before)
    before = jnp.where(info_ref[0, FIRST] == 1, zero, before)
    after = jnp.where(info_ref[0, LAST] == 1, zero, after)
    chans, span = before.shape[0], slabs_ref.shape[1]
    at = 0
    for part in [before] + own + [after]:
        done = 0
        while done < part.shape[1]:
            slab, column = divmod(at, span)
            take = min(span - column, part.shape[1] - done)
            slabs_ref[slab * chans : (slab + 1) * chans, column : column + take] = part[
                :, done : done + take
            ]
            done, at = done + take, at + take


def in_parts(ref):
    return [ref[:, at : at + HALO] for at in range(0, ref.shape[1], HALO)]


def ends_around(outer_ref, inner_ref):
    first, last = in_parts(outer_ref)
    return [first] + in_parts(inner_ref) + [last]


def live_mask(info_ref, rows):
    return lax.broadcasted_iota(jnp.int32, (1, rows), 1) < info_ref[0, LIVE]


def add_ends(info_ref, own, before, after):
    rows = own.shape[1]
    before = jnp.where(info_ref[0, FIRST] == 1, 0.0, before.astype(jnp.float32))
    after = jnp.where(info_ref[0, LAST] == 1, 0.0, after.astype(jnp.float32))
    return jnp.concatenate(
        [
            own[:, :HALO] + before,
            own[:, HALO : rows - HALO],
            own[:, rows - HALO :] + after,
        ],
        axis=1,
    )


def spread_kernel(
    child_hbm, down_hbm, grad_hbm, own_ref, next_ref, terms_ref, child_ref, down_ref, grad_ref, sems
):
    copies = [
        pltpu.make_async_copy(source, target, sems.at[i])
        for i, (source, target) in enumerate(
            ((child_hbm, child_ref), (down_hbm, down_ref), (grad_hbm, grad_ref))
        )
    ]
    for copy in copies:
        copy.start()
    for copy in copies:
        copy.wait()
    kids, chans, wide = down_ref.shape
    rows = own_ref.shape[1]
    slabs = (rows + HALO) // DOWN_SPAN
    total = jnp.zeros((slabs * chans, DOWN_SPAN), jnp.float32)
    terms = nt(down_ref[...].reshape(kids * chans, wide), grad_ref[...]).astype(jnp.bfloat16)
    for j in range(kids):
        index = child_ref[j : j + 1, :]
        index = jnp.where(index < rows + HALO, index, -1)
        total += spread_rows(terms_ref, terms[j * chans : (j + 1) * chans], index, slabs, DOWN_SPAN)
    for s in range(slabs - 1):
        own_ref[:, s * DOWN_SPAN : (s + 1) * DOWN_SPAN] = total[s * chans : (s + 1) * chans]
    next_ref[...] = total[(slabs - 1) * chans :].astype(next_ref.dtype)


def first_part(info_ref, map_ref, weight_ref, field_ref, slabs_ref, first_ref, slope_ref, taken_ref, blocks):
    pre = conv(info_ref, map_ref, weight_ref, slabs_ref, taken_ref, in_parts(field_ref), blocks)
    alive = live_mask(info_ref, map_ref.shape[2])
    for place, block in enumerate(blocks):
        part = slice(place * HALO, (place + 1) * HALO)
        lives = alive[:, block * HALO : (block + 1) * HALO]
        value = pre[:, part]
        first_ref[:, part] = jnp.where(lives, jax.nn.silu(value), 0.0).astype(jnp.bfloat16)
        slope_ref[:, part] = jnp.where(lives, silu_slope(value), 0.0)


def outer_kernel(
    info_ref,
    map_ref,
    weight_ref,
    field_ref,
    before_ref,
    after_ref,
    spread_ref,
    first_ref,
    slope_ref,
    taken_ref,
    to_next_ref,
    slabs_ref,
):
    put_window(slabs_ref, info_ref, before_ref[...], in_parts(field_ref), after_ref[...])
    blocks = [0, field_ref.shape[1] // HALO - 1]
    first_part(
        info_ref, map_ref, weight_ref, field_ref, slabs_ref, first_ref, slope_ref, taken_ref, blocks
    )
    chans = field_ref.shape[0]
    to_next_ref[:chans] = first_ref[:, HALO:]
    to_next_ref[chans:] = spread_ref[...]


def inner_kernel(
    info_ref,
    map_ref,
    weight_ref,
    field_ref,
    before_ref,
    after_ref,
    first_ref,
    slope_ref,
    taken_ref,
    slabs_ref,
):
    put_window(slabs_ref, info_ref, before_ref[...], in_parts(field_ref), after_ref[...])
    blocks = list(range(1, field_ref.shape[1] // HALO - 1))
    first_part(
        info_ref, map_ref, weight_ref, field_ref, slabs_ref, first_ref, slope_ref, taken_ref, blocks
    )


def second_kernel(
    info_ref,
    map_ref,
    weight_ref,
    outer_ref,
    inner_ref,
    before_ref,
    after_ref,
    field_ref,
    rows_ref,
    second_ref,
    d_second_ref,
    grad_weight_ref,
    to_prev_ref,
    to_next_ref,
    slabs_ref,
    taken_ref,
    terms_ref,
    sums_ref,
):
    chans, rows = field_ref.shape
    own = ends_around(outer_ref, inner_ref)
    put_window(slabs_ref, info_ref, before_ref[:chans], own, after_ref[...])
    blocks = list(range(rows // HALO))
    pre = conv(info_ref, map_ref, weight_ref, slabs_ref, taken_ref, own, blocks) + field_ref[...].astype(jnp.float32)
    alive = live_mask(info_ref, rows)
    second_ref[...] = jnp.where(alive, jax.nn.silu(pre), 0.0).astype(jnp.bfloat16)
    slope = jnp.where(alive, silu_slope(pre), 0.0)
    returned = jnp.where(info_ref[0, FIRST] == 1, 0.0, before_ref[chans:].astype(jnp.float32))
    grad_rows = jnp.concatenate([rows_ref[:, :HALO] + returned, rows_ref[:, HALO:]], axis=1)
    d_second_ref[...] = (grad_rows * slope).astype(jnp.bfloat16)
    grad_weight_ref[...] = nt(d_second_ref[...], taken_ref[...])
    ends = conv_back(
        map_ref, weight_ref, d_second_ref, terms_ref, sums_ref, True, 0, map_ref.shape[0]
    )
    half = len(ends) // 2
    to_prev_ref[:chans] = jnp.concatenate(ends[:half], axis=1).astype(to_prev_ref.dtype)
    to_prev_ref[chans:] = second_ref[:, :HALO]
    to_next_ref[...] = jnp.concatenate(ends[half:], axis=1).astype(to_next_ref.dtype)


def own_kernel(begin, end, map_ref, weight_ref, grad_ref, own_ref, terms_ref, sums_ref):
    parts = conv_back(map_ref, weight_ref, grad_ref, terms_ref, sums_ref, False, begin, end)
    for s, part in enumerate(parts):
        own_ref[:, s * SPREAD_SPAN : (s + 1) * SPREAD_SPAN] = part


def low_kernel(
    begin, end, map_ref, weight_ref, grad_ref, kids_ref, down_ref, own_ref, coarse_ref, terms_ref, sums_ref
):
    own_kernel(begin, end, map_ref, weight_ref, grad_ref, own_ref, terms_ref, sums_ref)
    kids, chans, wide = down_ref.shape
    flat = down_ref[...].reshape(kids * chans, wide)
    coarse_ref[...] = nn(kids_ref[...].T, flat).astype(jnp.bfloat16)


def ends_kernel(map_ref, weight_ref, grad_ref, to_prev_ref, to_next_ref, terms_ref, sums_ref):
    ends = conv_back(map_ref, weight_ref, grad_ref, terms_ref, sums_ref, True, 0, map_ref.shape[0])
    half = len(ends) // 2
    for ref, parts in ((to_prev_ref, ends[:half]), (to_next_ref, ends[half:])):
        stack_to_row(ref, jnp.concatenate(parts, axis=1).astype(ref.dtype))


def stack_to_row(ref, value):
    group, width = ref.shape[0], value.shape[1]
    for i in range(value.shape[0] // group):
        ref[:, i * width : (i + 1) * width] = value[i * group : (i + 1) * group]


def row_to_stack(ref, chans):
    width = ref.shape[1] * ref.shape[0] // chans
    return jnp.concatenate([ref[:, i : i + width] for i in range(0, ref.shape[1], width)], axis=0)


def middle_kernel(
    info_ref,
    child_ref,
    down_ref,
    grad_ref,
    second_ref,
    from_next_ref,
    from_prev_ref,
    rows_ref,
    slope_outer_ref,
    slope_inner_ref,
    taken_outer_ref,
    taken_inner_ref,
    grad_second_ref,
    d_first_ref,
    grads_ref,
    kids_ref,
    slabs_ref,
):
    kids, chans, wide = down_ref.shape
    rows = second_ref.shape[1]
    for s in range(rows // DOWN_SPAN):
        slabs_ref[s * chans : (s + 1) * chans, :] = second_ref[:, s * DOWN_SPAN : (s + 1) * DOWN_SPAN]
    after = from_next_ref[chans:]
    slabs_ref[rows // DOWN_SPAN * chans :, :] = jnp.where(
        info_ref[0, LAST] == 1, jnp.zeros_like(after), after
    )
    for j in range(kids):
        index = child_ref[j : j + 1, :]
        index = jnp.where(index < rows + HALO, index, -1)
        kids_ref[j * chans : (j + 1) * chans, :] = read_rows(slabs_ref[...], index, chans)
    grad_down = nn(kids_ref[...], grad_ref[...])
    slope = jnp.concatenate(ends_around(slope_outer_ref, slope_inner_ref), axis=1)
    d_first = (
        add_ends(info_ref, rows_ref[...], from_prev_ref[...], from_next_ref[:chans]) * slope
    ).astype(jnp.bfloat16)
    d_first_ref[...] = d_first
    d_outer = jnp.concatenate([d_first[:, :HALO], d_first[:, rows - HALO :]], axis=1)
    size = grad_second_ref.shape[1]
    grads_ref[:, :size] = grad_second_ref[...]
    grads_ref[:, size : 2 * size] = nt(d_outer, taken_outer_ref[...]) + nt(
        d_first[:, HALO : rows - HALO], taken_inner_ref[...]
    )
    for j in range(kids):
        grads_ref[:, 2 * size + j * wide : 2 * size + (j + 1) * wide] = grad_down[
            j * chans : (j + 1) * chans
        ]


def field_kernel(info_ref, low_ref, high_ref, d_second_ref, before_ref, after_ref, field_ref):
    chans = low_ref.shape[0]
    before, after = row_to_stack(before_ref, chans), row_to_stack(after_ref, chans)
    total = add_ends(info_ref, low_ref[...] + high_ref[...], before, after)
    field_ref[...] = (total + d_second_ref[...].astype(jnp.float32)).astype(jnp.bfloat16)


def last_kernel(info_ref, *refs):
    quarters, (first_ref, second_ref, down_ref, grads_ref) = refs[:-4], refs[-4:]
    share = quarters[0].shape[0]
    for step, quarter_ref in enumerate(quarters):
        at = (info_ref[0, DP] ^ step) * share if len(quarters) > 1 else 0
        grads_ref[pl.ds(pl.multiple_of(at, ROW), share), :] = quarter_ref[...]
    count, chans = first_ref.shape[0], first_ref.shape[1]
    kids, wide = down_ref.shape[0], down_ref.shape[2]
    size = count * chans
    second = grads_ref[:, :size].T
    first = grads_ref[:, size : 2 * size].T
    for k in range(count):
        second_ref[k] = second[k * chans : (k + 1) * chans]
        first_ref[k] = first[k * chans : (k + 1) * chans]
    for j in range(kids):
        down_ref[j] = grads_ref[:, 2 * size + j * wide : 2 * size + (j + 1) * wide]


def shape(dims, dtype):
    return jax.ShapeDtypeStruct(dims, dtype)


def call(kernel, outs, scratch, flops, *args, where=pltpu.VMEM, limit=VMEM_BYTES):
    smem = pl.BlockSpec(memory_space=pltpu.SMEM)
    vmem = pl.BlockSpec(memory_space=pltpu.VMEM)
    return pl.pallas_call(
        kernel,
        out_shape=outs,
        in_specs=[smem if a.shape == (1, 4) else pl.BlockSpec(memory_space=where) for a in args],
        out_specs=[vmem] * len(outs),
        scratch_shapes=scratch,
        compiler_params=pltpu.CompilerParams(vmem_limit_bytes=limit),
        cost_estimate=pl.CostEstimate(flops=flops, bytes_accessed=2**20, transcendentals=0),
    )(*args)


def shifted(value, axis, steps):
    count = lax.axis_size(axis)
    return lax.ppermute(value, axis, [(i, (i + steps) % count) for i in range(count)])


def body(
    features, kernel_map, child_map, live_rows, weight_first, weight_second, weight_down, out_grad
):
    bf16, f32 = jnp.bfloat16, jnp.float32
    field = features[0].T
    chans, rows = field.shape
    count = kernel_map.shape[1]
    offsets = kernel_map.reshape(count, 1, rows)
    children = child_map[0]
    kids, coarse = children.shape
    wide = weight_down.shape[2]
    grad_out = out_grad[0]
    place = lax.axis_index("space")
    devices = lax.axis_size("space")
    info = jnp.stack(
        [
            live_rows[0, 0],
            (place == 0).astype(jnp.int32),
            (place == devices - 1).astype(jnp.int32),
            lax.axis_index("dp").astype(jnp.int32),
        ]
    ).reshape(1, 4)
    window = rows + 2 * HALO
    flops = 2 * count * window * chans * rows
    down_slabs = (rows + HALO) // DOWN_SPAN
    slabs_scratch = pltpu.VMEM((READ_SLABS * chans, window // READ_SLABS), bf16)

    def back_scratch(width, offset_count):
        slabs = width // SPREAD_SPAN
        return [
            pltpu.VMEM((slabs * chans, rows), bf16),
            pltpu.VMEM((slabs, offset_count * chans, SPREAD_SPAN), bf16),
        ]

    before = shifted(field[:, rows - HALO :], "space", 1)
    after = shifted(field[:, :HALO], "space", -1)
    grad_rows, spread_next = call(
        spread_kernel,
        [shape((chans, rows), f32), shape((chans, HALO), bf16)],
        [
            pltpu.VMEM((down_slabs * chans, coarse), bf16),
            pltpu.VMEM(children.shape, jnp.int32),
            pltpu.VMEM(weight_down.shape, bf16),
            pltpu.VMEM(grad_out.shape, bf16),
            pltpu.SemaphoreType.DMA((3,)),
        ],
        2 * kids * (rows + HALO) * chans * coarse,
        children,
        weight_down,
        grad_out,
        where=pltpu.HBM,
        limit=60 * 2**20,
    )
    first_outer, slope_outer, taken_outer, to_next = call(
        outer_kernel,
        [
            shape((chans, 2 * HALO), bf16),
            shape((chans, 2 * HALO), f32),
            shape((count * chans, 2 * HALO), bf16),
            shape((2 * chans, HALO), bf16),
        ],
        [slabs_scratch],
        flops * 2 // 3,
        info,
        offsets,
        weight_first,
        field,
        before,
        after,
        spread_next,
    )
    before, after, first_outer, to_next = lax.optimization_barrier((before, after, first_outer, to_next))
    first_inner, slope_inner, taken_inner = call(
        inner_kernel,
        [
            shape((chans, rows - 2 * HALO), bf16),
            shape((chans, rows - 2 * HALO), f32),
            shape((count * chans, rows - 2 * HALO), bf16),
        ],
        [slabs_scratch],
        flops // 3,
        info,
        offsets,
        weight_first,
        field,
        before,
        after,
    )
    before = shifted(to_next, "space", 1)
    after = shifted(first_outer[:, :HALO], "space", -1)
    second, d_second, grad_second, to_prev, to_next = call(
        second_kernel,
        [
            shape((chans, rows), bf16),
            shape((chans, rows), bf16),
            shape((chans, count * chans), f32),
            shape((2 * chans, HALO), bf16),
            shape((chans, HALO), bf16),
        ],
        [slabs_scratch, pltpu.VMEM((count * chans, rows), bf16)]
        + back_scratch(2 * HALO, count),
        flops * 3 // 2,
        info,
        offsets,
        weight_second,
        first_outer,
        first_inner,
        before,
        after,
        field,
        grad_rows,
    )
    from_next = shifted(to_prev, "space", -1)
    from_prev = shifted(to_next, "space", 1)
    (own,) = call(
        functools.partial(own_kernel, 0, count),
        [shape((chans, rows), f32)],
        back_scratch(rows, count),
        flops // 2,
        offsets,
        weight_second,
        d_second,
    )
    d_first, grads, kid_rows = call(
        middle_kernel,
        [
            shape((chans, rows), bf16),
            shape((chans, 2 * count * chans + kids * wide), f32),
            shape((kids * chans, coarse), bf16),
        ],
        [pltpu.VMEM((down_slabs * chans, DOWN_SPAN), bf16)],
        2 * kids * (rows + HALO) * chans * coarse,
        info,
        children,
        weight_down,
        grad_out,
        second,
        from_next,
        from_prev,
        own,
        slope_outer,
        slope_inner,
        taken_outer,
        taken_inner,
        grad_second,
    )
    samples = lax.axis_size("dp")
    direct = samples == 4 and devices == 4 and chans // samples == ROW
    scale = float(samples * devices * rows) ** (-0.5)
    me = lax.axis_index("dp")
    share = chans // samples

    def partner(value, step):
        return lax.ppermute(value, "dp", [(i, i ^ step) for i in range(samples)])

    def quarter(step):
        return lax.dynamic_slice_in_dim(grads, (me ^ step) * share, share, axis=0)

    if direct:
        sent = [quarter(s).astype(bf16) for s in range(1, samples)]
        sent, d_first = lax.optimization_barrier((sent, d_first))
        got = [partner(v, s + 1) for s, v in enumerate(sent)]
    to_prev, to_next = call(
        ends_kernel,
        [shape((ROW, chans // ROW * HALO), bf16), shape((ROW, chans // ROW * HALO), bf16)],
        back_scratch(2 * HALO, count),
        flops // 2,
        offsets,
        weight_first,
        d_first,
    )
    if direct:
        got, to_prev, to_next = lax.optimization_barrier((got, to_prev, to_next))
        sent = (quarter(0) + sum(v.astype(f32) for v in got)).astype(bf16)
        sent, d_first = lax.optimization_barrier((sent, d_first))
        forth = shifted(jnp.concatenate([sent, to_next], axis=1), "space", 1)
        back = shifted(jnp.concatenate([sent, to_prev], axis=1), "space", -1)
        across = shifted(sent, "space", 2)
    else:
        after = shifted(to_prev, "space", -1)
        before = shifted(to_next, "space", 1)
    low, coarse_out = call(
        functools.partial(low_kernel, 0, LOW),
        [shape((chans, rows), f32), shape((coarse, wide), bf16)],
        back_scratch(rows, LOW),
        flops // 3,
        offsets,
        weight_first,
        d_first,
        kid_rows,
        weight_down,
    )
    if direct:
        forth, back, across, low = lax.optimization_barrier((forth, back, across, low))
        width = grads.shape[1]
        before, after = forth[:, width:], back[:, width:]
        even = sent.astype(f32) + across.astype(f32)
        odd = forth[:, :width].astype(f32) + back[:, :width].astype(f32)
        part = ((even + odd) * scale).astype(bf16)
        part, d_first = lax.optimization_barrier((part, d_first))
        parts = [part, partner(part, 1), partner(part, 2)]
    (high,) = call(
        functools.partial(own_kernel, LOW, count),
        [shape((chans, rows), f32)],
        back_scratch(rows, count - LOW),
        flops // 6,
        offsets,
        weight_first,
        d_first,
    )
    if direct:
        parts, high = lax.optimization_barrier((parts, high))
        parts.append(partner(parts[2], 1))
    else:
        parts = [(lax.psum(grads, ("space", "dp")) * scale).astype(bf16)]
    (feature_grad,) = call(
        field_kernel,
        [shape((chans, rows), bf16)],
        [],
        chans * rows,
        info,
        low,
        high,
        d_second,
        before,
        after,
    )
    out_first, out_second, out_down = call(
        last_kernel,
        [
            shape(weight_first.shape, bf16),
            shape(weight_second.shape, bf16),
            shape(weight_down.shape, bf16),
        ],
        [pltpu.VMEM(grads.shape, bf16)],
        1,
        info,
        *parts,
    )
    return (coarse_out[None], feature_grad.T[None], out_first, out_second, out_down)


def solution(mesh):
    placed = (
        P(("groups", "dp"), "space", None),
        P(("groups", "dp"), None, "space"),
        P(("groups", "dp"), None, "space"),
        P(("groups", "dp"), "space"),
        P(),
        P(),
        P(),
        P(("groups", "dp"), "space", None),
    )
    return jax.shard_map(
        body,
        mesh=mesh,
        in_specs=placed,
        out_specs=(
            P(("groups", "dp"), "space", None),
            P(("groups", "dp"), "space", None),
            P("groups", None, None),
            P("groups", None, None),
            P("groups", None, None),
        ),
        check_vma=False,
    )
```
